128 devices in a mesh: ctx: 32 (over y, z, core), head: 4 (over x).
Axes of the slice: x: 4, y: 4, z: 4, core: 2. Of those that a mesh axis runs over, the one named last changes fastest.
Arguments:
- token_ids: int32 [4096], P('ctx'), may hold values from 0 to 16383
- targets: int32 [4096], P(('ctx', 'head')), may hold values from 0 to 16383
- embed: bfloat16 [16384, 4096], P('head', 'ctx'), may hold values from -6 to 6
- w_zx: bfloat16 [4096, 2, 4096], P(None, None, 'head'), may hold values from -0.09375 to 0.09375
- w_bc: bfloat16 [4096, 2, 512], P(None, None, 'head'), may hold values from -0.09375 to 0.09375
- w_dt: bfloat16 [4096, 64], P(None, 'head'), may hold values from -0.21875 to 0.21875
- conv_x: float32 [4, 4096], P(None, 'head'), may hold values from -3 to 3
- conv_bc: float32 [4, 2, 512], P(None, None, 'head'), may hold values from -3 to 3
- dt_bias: float32 [64], P('head'), may hold values from -7 to 0.2
- a_log: float32 [64], P('head')
- d_skip: float32 [64], P('head'), may hold values from 0.3 to 4
- norm_gain: float32 [4096], P('head'), may hold values from 0.1 to 1.9
- pre_gain: float32 [4096], replicated, may hold values from 0.1 to 1.9
- final_gain: float32 [4096], replicated, may hold values from 0.1 to 1.9
- w_out: bfloat16 [4096, 4096], P('head', 'ctx'), may hold values from -0.09375 to 0.09375
- lm_head: bfloat16 [4096, 16384], P('head', 'ctx'), as said below
Outputs:
- scores: float32 [4096], P(('ctx', 'head'))
The draws below stay inside these ranges and needn't reach their ends.
Inputs may be any that keep to these rules, and one draw needn't show every extreme that they name: `lm_head`: vocabulary projection, every entry within 552 / sqrt(4096) in magnitude.
All inputs are finite; a program needn't handle non-finite values.
Results may differ from the reference program's by a relative error of at most 0.038.
Values may be sent and summed in bfloat16 or wider, within the bound.
No kernel may reach another device: no remote copies, remote signals or barrier semaphores. Data moves between devices by JAX's collectives and lax.ppermute only.
A program may use at most 128 MiB of HBM per device.

```python
import math
import jax
import jax.numpy as jnp
import numpy as np
from jax import lax

D = 4096
V = 16384
HEADS = 64
HEAD_DIM = 64
STATE = 128
GROUPS = 4
CONV = 4
TOK_DEV = 128
TOKENS = 4096


def head_kinds(key):
    coin_flip = jax.random.uniform(jax.random.fold_in(key, 11), (HEADS,))
    slow_share = 0.5
    is_slow = coin_flip < slow_share
    spread = jax.random.uniform(jax.random.fold_in(key, 12), (HEADS,), minval=0.5, maxval=1.5)
    return (is_slow, spread)


def draw_dt_bias(key, part):
    is_slow, spread = head_kinds(key)
    jitter = jax.random.uniform(jax.random.fold_in(key, 13), (HEADS,), minval=0.0, maxval=0.2)
    return (jnp.where(is_slow, -7.0, 0.0) + jitter).astype(jnp.float32)


def draw_a_log(key, part):
    is_slow, spread = head_kinds(key)
    decay_rate = jnp.where(is_slow, spread / (TOKENS * 0.02), 0.03 * spread)
    return jnp.log(decay_rate).astype(jnp.float32)


def clipped_normal(key, shape):
    return jnp.clip(jax.random.normal(key, shape, jnp.float32), -6.0, 6.0)


def draw_lm_head(key, part):
    columns = clipped_normal(jax.random.fold_in(key, 21), (D, V)) * (3.0 / D ** 0.5)
    return columns.astype(jnp.bfloat16)


def touch_ends(entries, rng, smallest, high):
    dims = entries.shape
    place = [jax.random.randint(jax.random.fold_in(rng, axis), (), 0, dims[axis]) for axis in range(len(dims))]
    entries = entries.at[tuple(place)].set(smallest)
    longest = dims.index(max(dims))
    place[longest] = (place[longest] + 1) % dims[longest]
    return entries.at[tuple(place)].set(high)


def block_levels(key, extent, shards, least, high):
    def one(dim, blocks):
        draws = jax.random.uniform(jax.random.fold_in(jax.random.fold_in(key, 6), dim), (blocks,), jnp.float32, least / len(shards), high / len(shards))
        return jnp.repeat(jnp.exp(draws), extent[dim] // blocks).reshape((-1,) + (1,) * (len(extent) - dim - 1))

    level = one(*shards[0])
    for cut in shards[1:]:
        level = level * one(*cut)
    return level


def rank_table(count, lean):
    loads = [(1 << 20) // math.isqrt(standing ** lean) + 1 for standing in range(1, count + 1)]
    width = 1 + sum(loads) // (1 << 30)
    return np.cumsum(np.array([max(1, weight // width) for weight in loads]))


def ranked_ids(key, shape, count, skew):
    table = rank_table(count, skew)
    lot = jax.random.randint(jax.random.fold_in(key, 1), shape, 0, int(table[count - 1]))
    grade = jnp.searchsorted(jnp.asarray(table, jnp.int32), lot, side="right")
    return jax.random.permutation(jax.random.fold_in(key, 2), count)[grade].astype(jnp.int32)


def noise(key, extent, scale, most, pieces=(), kind=jnp.bfloat16):
    result = scale * jax.random.normal(key, extent, jnp.float32)
    if pieces:
        result = result * block_levels(key, extent, pieces, -0.22, 0.18)
    return jnp.clip(result, -most, most).astype(kind)


def setup_inputs(seed: int = 0) -> dict:
    keys = jax.random.split(jax.random.key(seed), 17)
    return {
        "token_ids": touch_ends(ranked_ids(keys[0], (TOKENS,), V, 2), jax.random.fold_in(keys[0], 3), 0, V - 1).astype(jnp.int32),
        "targets": touch_ends(ranked_ids(keys[1], (TOKENS,), V, 2), jax.random.fold_in(keys[1], 3), 0, V - 1).astype(jnp.int32),
        "embed": noise(keys[2], (V, D), 1.0, 6.0, ((0, 4), (1, 32))),
        "w_zx": noise(keys[3], (D, 2, HEADS * HEAD_DIM), D ** -0.5, 0.09375, ((2, 4),)),
        "w_bc": noise(keys[4], (D, 2, GROUPS * STATE), D ** -0.5, 0.09375, ((2, 4),)),
        "w_dt": noise(keys[5], (D, HEADS), (D // 6) ** -0.5, 0.21875, ((1, 4),)),
        "conv_x": noise(keys[6], (CONV, HEADS * HEAD_DIM), 0.5, 3.0, ((1, 4),), jnp.float32),
        "conv_bc": noise(keys[7], (CONV, 2, GROUPS * STATE), 0.5, 3.0, ((2, 4),), jnp.float32),
        "dt_bias": draw_dt_bias(jax.random.fold_in(keys[16], 71), 0),
        "a_log": draw_a_log(jax.random.fold_in(keys[16], 71), 0),
        "d_skip": jnp.clip(jnp.exp(math.log(4.0) - 2.5902671 * jax.random.uniform(keys[10], (HEADS,), jnp.float32) ** block_levels(keys[10], (HEADS,), ((0, 4),), -0.2, 0.2)), 0.3, 4.0),
        "norm_gain": jnp.clip(1.0 + 0.18 * jax.random.normal(keys[11], (HEADS * HEAD_DIM,), jnp.float32), 0.1, 1.9),
        "pre_gain": jnp.clip(1.0 + 0.18 * jax.random.normal(keys[12], (D,), jnp.float32), 0.1, 1.9),
        "final_gain": jnp.clip(1.0 + 0.18 * jax.random.normal(keys[13], (D,), jnp.float32), 0.1, 1.9),
        "w_out": noise(keys[14], (HEADS * HEAD_DIM, D), (HEADS * HEAD_DIM) ** -0.5, 0.09375, ((0, 4), (1, 32))),
        "lm_head": draw_lm_head(jax.random.fold_in(keys[16], 71), 0),
    }


def norm_rows(values, gain):
    return values * lax.rsqrt(lax.optimization_barrier(jnp.mean(values * values, axis=-1, keepdims=True)) + 1e-05) * gain

def block_mixer(state_in, block):
    x_block, b_block, c_block, step_block, rate_block = block
    log_decay = jnp.cumsum(rate_block, axis=0)
    decay_gap = log_decay.T[:, :, None] - log_decay.T[:, None, :]
    positions = jnp.arange(log_decay.shape[0])
    causal = positions[:, None] >= positions[None, :]
    decay_mask = jnp.exp(jnp.where(causal[None], decay_gap, -jnp.inf))
    scores = jnp.einsum('thn,shn->hts', c_block, b_block, precision=lax.Precision.HIGHEST)
    mixing = scores * decay_mask * step_block.T[:, None, :]
    y_local = jnp.einsum('hts,shp->thp', mixing, x_block, precision=lax.Precision.HIGHEST)
    y_carry = jnp.einsum('thn,hpn->thp', c_block, state_in, precision=lax.Precision.HIGHEST) * jnp.exp(log_decay)[:, :, None]
    tail_decay = jnp.exp(log_decay[-1][None, :] - log_decay) * step_block
    end_state = jnp.einsum('sh,shp,shn->hpn', tail_decay, x_block, b_block, precision=lax.Precision.HIGHEST)
    new_state = jnp.exp(log_decay[-1])[:, None, None] * state_in + end_state
    return (new_state, y_local + y_carry)

def reference(token_ids, targets, embed, w_zx, w_bc, w_dt, conv_x, conv_bc, dt_bias, a_log, d_skip, norm_gain, pre_gain, final_gain, w_out, lm_head):
    embedded = jnp.take(embed, token_ids, axis=0)
    normed_in = norm_rows(embedded.astype(jnp.float32), pre_gain).astype(jnp.bfloat16)
    gate_z = jnp.dot(normed_in, w_zx[:, 0, :], preferred_element_type=jnp.float32)
    x_in = jnp.dot(normed_in, w_zx[:, 1, :], preferred_element_type=jnp.float32)
    b_in = jnp.dot(normed_in, w_bc[:, 0, :], preferred_element_type=jnp.float32)
    c_in = jnp.dot(normed_in, w_bc[:, 1, :], preferred_element_type=jnp.float32)
    step_raw = jnp.dot(normed_in, w_dt, preferred_element_type=jnp.float32)
    mixed_in = jnp.concatenate([x_in, b_in, c_in], axis=1)
    kernel = jnp.concatenate([conv_x, conv_bc[:, 0, :], conv_bc[:, 1, :]], axis=1)
    padded = jnp.concatenate([jnp.zeros((CONV - 1, mixed_in.shape[1]), jnp.float32), mixed_in], axis=0)
    convolved = jnp.zeros(mixed_in.shape, jnp.float32)
    for offset in range(CONV):
        convolved = convolved + kernel[offset] * padded[offset:offset + TOKENS]
    activated = jax.nn.silu(convolved)
    channels = HEADS * HEAD_DIM
    group_cols = GROUPS * STATE
    per_group = HEADS // GROUPS
    x_heads = activated[:, :channels].reshape(TOKENS, HEADS, HEAD_DIM)
    b_heads = jnp.repeat(activated[:, channels:channels + group_cols].reshape(TOKENS, GROUPS, STATE), per_group, axis=1)
    c_heads = jnp.repeat(activated[:, channels + group_cols:].reshape(TOKENS, GROUPS, STATE), per_group, axis=1)
    step_size = jax.nn.softplus(step_raw + dt_bias)
    log_rate = -jnp.exp(a_log) * step_size
    block_count = TOKENS // TOK_DEV

    def by_block(values):
        return values.reshape((block_count, TOK_DEV) + values.shape[1:])
    start_state = jnp.zeros((HEADS, HEAD_DIM, STATE), jnp.float32)
    final_state, y_blocks = lax.scan(block_mixer, start_state, (by_block(x_heads), by_block(b_heads), by_block(c_heads), by_block(step_size), by_block(log_rate)))
    mixer_out = y_blocks.reshape(TOKENS, HEADS, HEAD_DIM) + d_skip[None, :, None] * x_heads
    gated_raw = mixer_out.reshape(TOKENS, channels) * jax.nn.silu(gate_z)
    grouped = gated_raw.reshape(TOKENS, GROUPS, channels // GROUPS)
    grouped = grouped * lax.rsqrt(lax.optimization_barrier(jnp.mean(grouped * grouped, axis=-1, keepdims=True)) + 1e-05)
    gated = (grouped.reshape(TOKENS, channels) * norm_gain).astype(jnp.bfloat16)
    residual = (embedded.astype(jnp.float32) + jnp.dot(gated, w_out, preferred_element_type=jnp.float32)).astype(jnp.bfloat16)
    normed_out = norm_rows(residual.astype(jnp.float32), final_gain).astype(jnp.bfloat16)

    def score_block(block):
        row_block, target_block = block
        logits = jnp.dot(row_block, lm_head, preferred_element_type=jnp.float32)
        softmax_p = jax.nn.softmax(logits, axis=-1)
        mean_logit = lax.optimization_barrier(jnp.sum(softmax_p * logits, axis=-1))
        centered = logits - mean_logit[:, None]
        spread = lax.optimization_barrier(jnp.sum(softmax_p * centered * centered, axis=-1))
        picked = jnp.take_along_axis(logits, target_block[:, None].astype(jnp.int32), axis=1)[:, 0]
        return (picked - mean_logit) * lax.rsqrt(jnp.maximum(spread, 0.25))
    scores = lax.map(score_block, (normed_out.reshape(block_count, TOK_DEV, D), targets.reshape(block_count, TOK_DEV)))
    return scores.reshape(TOKENS)
```

```python
import jax
import jax.numpy as jnp
from jax import lax
from jax.experimental import pallas as pl
from jax.experimental.pallas import tpu as pltpu
from jax.sharding import PartitionSpec as P

HEAD_DIM = 64
STATE = 128


exact_prec = lax.Precision.HIGHEST


def shift_head(by):
    return "head", [(i, (i + by) % 4) for i in range(4)]


def shift_mixed(first):
    def shift(by):
        pairs = []
        for i in range(32):
            y, z, core = i // 8, (i // 2) % 4, i % 2
            if (core == 0) == first:
                z = (z + by) % 4
            else:
                y = (y + by) % 4
            pairs.append((i, y * 8 + z * 2 + core))
        return "ctx", pairs

    return shift


def swap_core(value):
    return lax.ppermute(value, "ctx", [(i, i ^ 1) for i in range(32)])


def moved(value, shift, by):
    axis, pairs = shift(by)
    return lax.ppermute(value, axis, pairs)


def passed_along(value, axis, by):
    length = lax.axis_size(axis)
    pairs = [(i, i + by) for i in range(length) if 0 <= i + by < length]
    return lax.ppermute(value, axis, pairs)


def ring_gather(value, shift):
    half = value.shape[0] // 2
    left = moved(value, shift, 1)
    right = moved(value, shift, -1)
    far_low = moved(left[:half], shift, 1)
    far_high = moved(right[half:], shift, -1)
    return value, right, jnp.concatenate([far_low, far_high]), left


def ring_reduce(parts, shift):
    own, ahead, far, behind = parts
    half = own.shape[0] // 2
    from_left = moved(far[:half], shift, 1)
    from_right = moved(far[half:], shift, -1)
    ahead = jnp.concatenate([ahead[:half] + from_left, ahead[half:]])
    behind = jnp.concatenate([behind[:half], behind[half:] + from_right])
    left = moved(ahead, shift, 1)
    right = moved(behind, shift, -1)
    f32 = jnp.float32
    return own.astype(f32) + left.astype(f32) + right.astype(f32)


def look_up(ids, table):
    count, (table_rows, cols) = ids.shape[0], table.shape
    depth, block = 512, 1024
    parts = table_rows // depth
    bf16, f32 = jnp.bfloat16, jnp.float32

    def kernel(ids_ref, table_ref, out_ref):
        lane = lax.broadcasted_iota(jnp.int32, (128, 128), 1)
        for r in range(block // 128):
            column = jnp.broadcast_to(ids_ref[0, r : r + 1, :], (128, 128)).T
            low = jnp.bitwise_and(column, depth - 1)
            rest = jnp.right_shift(column, depth.bit_length() - 1)
            picks = [(low == lane + 128 * c).astype(f32).astype(bf16) for c in range(depth // 128)]
            found = jnp.dot(
                jnp.concatenate(picks, axis=1), table_ref[...], preferred_element_type=f32
            )
            chosen = jnp.zeros((128, cols), f32)
            for g in range(parts):
                chosen = jnp.where(rest == g, found[:, g * cols : (g + 1) * cols], chosen)
            out_ref[r * 128 : (r + 1) * 128, :] = chosen.astype(bf16)

    side_by_side = table.reshape(parts, depth, cols).transpose(1, 0, 2).reshape(depth, parts * cols)
    return pl.pallas_call(
        kernel,
        grid=(count // block,),
        in_specs=[
            pl.BlockSpec((1, block // 128, 128), lambda i: (i, 0, 0)),
            pl.BlockSpec((depth, parts * cols), lambda i: (0, 0)),
        ],
        out_specs=pl.BlockSpec((block, cols), lambda i: (i, 0)),
        out_shape=jax.ShapeDtypeStruct((count, cols), bf16),
        compiler_params=pltpu.CompilerParams(vmem_limit_bytes=24 << 20),
        cost_estimate=pl.CostEstimate(
            flops=2 * count * table_rows * cols, bytes_accessed=4 << 20, transcendentals=0
        ),
    )(ids.reshape(count // block, block // 128, 128), side_by_side)


def project(rows, w_zx, w_bc, w_dt):
    count, width = rows.shape
    channels, group_cols, heads = w_zx.shape[2], w_bc.shape[2], w_dt.shape[1]
    depth = 1024
    f32 = jnp.float32

    def kernel(rows_ref, zx_ref, bc_ref, dt_ref, z_out, x_out, bc_out, dt_out):
        @pl.when(pl.program_id(0) == 0)
        def _():
            for out in (z_out, x_out, bc_out, dt_out):
                out[...] = jnp.zeros_like(out)

        part = rows_ref[...]
        zx = zx_ref[...].reshape(depth, 2 * channels)
        z_out[...] += jnp.dot(part, zx[:, :channels], preferred_element_type=f32)
        x_out[...] += jnp.dot(part, zx[:, channels:], preferred_element_type=f32)
        bc = bc_ref[...].reshape(depth, 2 * group_cols)
        bc_out[...] += jnp.dot(part, bc, preferred_element_type=f32)
        dt_out[...] += jnp.dot(part, dt_ref[...], preferred_element_type=f32)

    widths = (channels, channels, 2 * group_cols, heads)
    return pl.pallas_call(
        kernel,
        grid=(width // depth,),
        in_specs=[
            pl.BlockSpec((count, depth), lambda i: (0, i)),
            pl.BlockSpec((depth, 2, channels), lambda i: (i, 0, 0)),
            pl.BlockSpec((depth, 2, group_cols), lambda i: (i, 0, 0)),
            pl.BlockSpec((depth, heads), lambda i: (i, 0)),
        ],
        out_specs=[pl.BlockSpec((count, n), lambda i: (0, 0)) for n in widths],
        out_shape=[jax.ShapeDtypeStruct((count, n), f32) for n in widths],
        compiler_params=pltpu.CompilerParams(vmem_limit_bytes=40 << 20),
        cost_estimate=pl.CostEstimate(
            flops=2 * count * width * sum(widths),
            bytes_accessed=2 * width * sum(widths),
            transcendentals=0,
        ),
    )(rows, w_zx, w_bc, w_dt)


def rms_scale(values, gain):
    return values * lax.rsqrt(jnp.mean(values * values, axis=-1, keepdims=True) + 1e-05) * gain


def join_stats(left_set, right_set):
    peak_left, sum_left, first_left, second_left, target_left = left_set
    peak_right, sum_right, first_right, second_right, target_right = right_set
    row_peak = jnp.maximum(peak_left, peak_right)
    shift_left = peak_left - row_peak
    shift_right = peak_right - row_peak
    weight_left = jnp.exp(shift_left)
    weight_right = jnp.exp(shift_right)
    exp_sum = weight_left * sum_left + weight_right * sum_right
    first_moment = weight_left * (first_left + shift_left * sum_left) + weight_right * (
        first_right + shift_right * sum_right
    )
    second_moment = weight_left * (
        second_left + 2.0 * shift_left * first_left + shift_left * shift_left * sum_left
    ) + weight_right * (
        second_right + 2.0 * shift_right * first_right + shift_right * shift_right * sum_right
    )
    return (row_peak, exp_sum, first_moment, second_moment, target_left + target_right)


def vocab_stats(rows, row_targets, tables):
    logits = jnp.concatenate(
        [jnp.dot(rows, table, preferred_element_type=jnp.float32) for table, _ in tables], axis=1
    )
    vocab_ids = jnp.concatenate([ids for _, ids in tables])
    row_peak = jnp.max(logits, axis=1)
    shifted = logits - row_peak[:, None]
    weights = jnp.exp(shifted)
    is_target = row_targets[:, None] == vocab_ids[None, :]
    return jnp.stack(
        [
            row_peak,
            jnp.sum(weights, axis=1),
            jnp.sum(weights * shifted, axis=1),
            jnp.sum(weights * shifted * shifted, axis=1),
            jnp.sum(jnp.where(is_target, logits, 0.0), axis=1),
        ]
    )


def on_device(
    token_ids,
    targets,
    embed,
    w_zx,
    w_bc,
    w_dt,
    conv_x,
    conv_bc,
    dt_bias,
    a_log,
    d_skip,
    norm_gain,
    pre_gain,
    final_gain,
    w_out,
    lm_head,
):
    bf16, f32 = jnp.bfloat16, jnp.float32
    ctx_count = lax.axis_size("ctx")
    head_count = lax.axis_size("head")
    tok_rows = token_ids.shape[0]
    quarter = tok_rows // head_count
    model_width = pre_gain.shape[0]
    head_pos = lax.axis_index("head")
    ctx_pos = lax.axis_index("ctx")
    w_out_full = lax.all_gather(w_out, "ctx", axis=1, tiled=True)

    packed = jnp.concatenate([token_ids, targets])
    packed = jnp.broadcast_to(packed[None], (ctx_count, tok_rows + quarter))
    packed = lax.all_to_all(packed, "ctx", 0, 0, tiled=True)
    all_ids = packed[:, :tok_rows].reshape(ctx_count, head_count, quarter)
    group_targets = packed[:, tok_rows:]

    table_rows, slice_cols = embed.shape
    by_owner = jnp.roll(all_ids, -head_pos, axis=1).transpose(1, 0, 2)
    local_ids = by_owner.reshape(-1) - head_pos * table_rows
    looked = look_up(local_ids, embed)
    looked = looked.reshape(head_count, ctx_count * quarter, slice_cols)
    mine = ring_reduce([looked[k] for k in range(4)], shift_head).astype(bf16)
    mine = mine.reshape(ctx_count, quarter, slice_cols)
    own_emb = lax.all_to_all(mine, "ctx", split_axis=0, concat_axis=2, tiled=True)
    own_emb = own_emb.reshape(quarter, model_width)
    normed_own = rms_scale(own_emb.astype(f32), pre_gain).astype(bf16)
    normed_in = jnp.zeros((tok_rows, model_width), bf16)
    for ahead, block in enumerate(ring_gather(normed_own, shift_head)):
        row = ((head_pos + ahead) % head_count) * quarter
        normed_in = lax.dynamic_update_slice_in_dim(normed_in, block, row, 0)

    normed_in, lm_head = lax.optimization_barrier((normed_in, lm_head))
    vocab_own = lax.all_gather(lm_head, "head", axis=0, tiled=True)
    vocab_other = swap_core(vocab_own)

    channels = w_zx.shape[2]
    group_cols = w_bc.shape[2]
    gate_z, proj_x, proj_bc, step_raw = project(normed_in, w_zx, w_bc, w_dt)
    mixed_in = jnp.concatenate([proj_x, proj_bc], axis=1)
    conv_taps = conv_x.shape[0]
    rim_rows = passed_along(mixed_in[tok_rows - conv_taps + 1 :], "ctx", 1)
    kernel = jnp.concatenate([conv_x, conv_bc.reshape(conv_taps, 2 * group_cols)], axis=1)
    extended = jnp.concatenate([rim_rows, mixed_in], axis=0)
    convolved = jnp.zeros_like(mixed_in)
    for offset in range(conv_taps):
        convolved = convolved + kernel[offset] * extended[offset : offset + tok_rows]
    activated = jax.nn.silu(convolved)
    heads = step_raw.shape[1]
    x_heads = activated[:, :channels].reshape(tok_rows, heads, HEAD_DIM)
    b_act = activated[:, channels : channels + group_cols]
    c_act = activated[:, channels + group_cols :]
    step_size = jax.nn.softplus(step_raw + dt_bias)
    log_rate = -jnp.exp(a_log) * step_size
    positions = jnp.arange(tok_rows)
    causal = positions[:, None] >= positions[None, :]
    log_decay = jnp.dot(causal.astype(f32), log_rate, precision=exact_prec)
    log_total = log_decay[-1]

    tail_decay = jnp.exp(log_total[None, :] - log_decay) * step_size
    end_state = jnp.einsum("sh,shp,sn->hpn", tail_decay, x_heads, b_act, precision=exact_prec)
    part_rows = heads * HEAD_DIM // ctx_count
    slices = end_state.astype(bf16).reshape(ctx_count, part_rows, STATE)
    first = log_total.astype(bf16)
    second = (log_total - first.astype(f32)).astype(bf16)
    third = (log_total - first.astype(f32) - second.astype(f32)).astype(bf16)
    totals = jnp.repeat(jnp.stack([first, second, third], axis=1), ctx_count // heads, axis=0)
    totals = jnp.broadcast_to(totals[:, :, None], (ctx_count, 3, STATE))
    totals = jnp.concatenate([totals, jnp.zeros((ctx_count, 13, STATE), bf16)], axis=1)
    message = jnp.concatenate([slices, totals], axis=1)
    arrived = lax.all_to_all(message, "ctx", 0, 0, tiled=True)
    block_logs = jnp.sum(arrived[:, part_rows : part_rows + 3, 0].astype(f32), axis=1)
    blocks = jnp.arange(ctx_count)
    earlier = blocks[:, None] > blocks[None, :]
    upto = jnp.sum(jnp.where(blocks[:, None] >= blocks[None, :], block_logs[None, :], 0.0), axis=1)
    gap = (upto - block_logs)[:, None] - upto[None, :]
    weigh = jnp.exp(jnp.where(earlier, gap, -jnp.inf))
    parts = arrived[:, :part_rows].astype(f32).reshape(ctx_count, part_rows * STATE)
    entering = jnp.dot(weigh, parts, precision=exact_prec).astype(bf16)
    entering = entering.reshape(ctx_count, part_rows, STATE)
    state_in = lax.all_to_all(entering, "ctx", 0, 0, tiled=True)
    state_in = state_in.reshape(heads, HEAD_DIM, STATE).astype(f32)

    decay_gap = log_decay.T[:, :, None] - log_decay.T[:, None, :]
    decay_mask = jnp.exp(jnp.where(causal[None], decay_gap, -jnp.inf))
    scores = jnp.einsum("tn,sn->ts", c_act, b_act, precision=exact_prec)
    mixing = scores[None] * decay_mask * step_size.T[:, None, :]
    y_local = jnp.einsum("hts,shp->thp", mixing, x_heads, precision=exact_prec)
    y_carry = (
        jnp.einsum("tn,hpn->thp", c_act, state_in, precision=exact_prec)
        * jnp.exp(log_decay)[:, :, None]
    )
    mixer_out = y_local + y_carry + d_skip[None, :, None] * x_heads
    gated_raw = mixer_out.reshape(tok_rows, channels) * jax.nn.silu(gate_z)
    gated_out = rms_scale(gated_raw, norm_gain).astype(bf16)

    partial_out = jnp.dot(gated_out, w_out_full, preferred_element_type=f32).astype(bf16)
    partial_out = partial_out.reshape(head_count, quarter, model_width)
    by_owner_out = jnp.roll(partial_out, -head_pos, axis=0)
    summed_out = ring_reduce([by_owner_out[k] for k in range(4)], shift_head)
    residual = (own_emb.astype(f32) + summed_out).astype(bf16)
    normed_out = rms_scale(residual.astype(f32), final_gain).astype(bf16)

    along_first, along_second = shift_mixed(True), shift_mixed(False)
    first_rows = jnp.stack(ring_gather(normed_out, along_first))
    all_rows = ring_gather(first_rows, along_second)
    y_pos, z_pos, core = ctx_pos // 8, (ctx_pos // 2) % 4, ctx_pos % 2
    by_chip = lax.dynamic_index_in_dim(group_targets.reshape(4, 4, 2, quarter), core, 2, False)
    by_chip = jnp.roll(by_chip, (-y_pos, -z_pos), (0, 1))
    by_chip = jnp.where(core == 0, by_chip, by_chip.transpose(1, 0, 2))
    vocab_width = vocab_own.shape[1]
    columns = jnp.arange(vocab_width, dtype=jnp.int32)
    tables = [
        (vocab_own, ctx_pos * vocab_width + columns),
        (vocab_other, (ctx_pos ^ 1) * vocab_width + columns),
    ]
    all_stats = [None] * 4
    for group in ((0,), (1, 3), (2,)):
        rows = jnp.concatenate([all_rows[k].reshape(-1, model_width) for k in group])
        wanted = jnp.concatenate([by_chip[k].reshape(-1) for k in group])
        stats = vocab_stats(rows, wanted, tables).reshape(5, len(group), 4, quarter)
        for place, k in enumerate(group):
            all_stats[k] = stats[:, place]
    merged = tuple(all_stats[0])
    for ahead in range(1, 4):
        merged = join_stats(merged, tuple(moved(all_stats[ahead], along_second, ahead)))
    both = jnp.stack(merged)
    merged = tuple(both[:, 0])
    for ahead in range(1, 4):
        merged = join_stats(merged, tuple(moved(both[:, ahead], along_first, ahead)))
    row_peak, exp_sum, first_moment, second_moment, target_logit = merged
    mean_shift = first_moment / exp_sum
    spread = second_moment / exp_sum - mean_shift * mean_shift
    return (target_logit - row_peak - mean_shift) * lax.rsqrt(jnp.maximum(spread, 0.25))


def solution(mesh):
    placed = (
        P("ctx"),
        P(("ctx", "head")),
        P("head", "ctx"),
        P(None, None, "head"),
        P(None, None, "head"),
        P(None, "head"),
        P(None, "head"),
        P(None, None, "head"),
        P("head"),
        P("head"),
        P("head"),
        P("head"),
        P(),
        P(),
        P("head", "ctx"),
        P("head", "ctx"),
    )
    return jax.shard_map(
        on_device, mesh=mesh, in_specs=placed, out_specs=P(("ctx", "head")), check_vma=False
    )
```

```python
import jax
import jax.numpy as jnp
from jax import lax
from jax.experimental import pallas as pl
from jax.experimental.pallas import tpu as pltpu
from jax.sharding import PartitionSpec as P

HEAD_DIM = 64
STATE = 128


exact_prec = lax.Precision.HIGHEST


def shift_head(by):
    return "head", [(i, (i + by) % 4) for i in range(4)]


def shift_mixed(first):
    def shift(by):
        pairs = []
        for i in range(32):
            y, z, core = i // 8, (i // 2) % 4, i % 2
            if (core == 0) == first:
                z = (z + by) % 4
            else:
                y = (y + by) % 4
            pairs.append((i, y * 8 + z * 2 + core))
        return "ctx", pairs

    return shift


def swap_core(value):
    return lax.ppermute(value, "ctx", [(i, i ^ 1) for i in range(32)])


def moved(value, shift, by):
    axis, pairs = shift(by)
    return lax.ppermute(value, axis, pairs)


def passed_along(value, axis, by):
    length = lax.axis_size(axis)
    pairs = [(i, i + by) for i in range(length) if 0 <= i + by < length]
    return lax.ppermute(value, axis, pairs)


def ring_gather(value, shift):
    half = value.shape[0] // 2
    left = moved(value, shift, 1)
    right = moved(value, shift, -1)
    far_low = moved(left[:half], shift, 1)
    far_high = moved(right[half:], shift, -1)
    return value, right, jnp.concatenate([far_low, far_high]), left


def ring_reduce(parts, shift):
    own, ahead, far, behind = parts
    half = own.shape[0] // 2
    from_left = moved(far[:half], shift, 1)
    from_right = moved(far[half:], shift, -1)
    ahead = jnp.concatenate([ahead[:half] + from_left, ahead[half:]])
    behind = jnp.concatenate([behind[:half], behind[half:] + from_right])
    left = moved(ahead, shift, 1)
    right = moved(behind, shift, -1)
    f32 = jnp.float32
    return own.astype(f32) + left.astype(f32) + right.astype(f32)


def look_up(ids, table):
    count, (table_rows, cols) = ids.shape[0], table.shape
    depth, block = 512, 1024
    parts = table_rows // depth
    bf16, f32 = jnp.bfloat16, jnp.float32

    def kernel(ids_ref, table_ref, out_ref):
        lane = lax.broadcasted_iota(jnp.int32, (128, 128), 1)
        for r in range(block // 128):
            column = jnp.broadcast_to(ids_ref[0, r : r + 1, :], (128, 128)).T
            low = jnp.bitwise_and(column, depth - 1)
            rest = jnp.right_shift(column, depth.bit_length() - 1)
            picks = [(low == lane + 128 * c).astype(f32).astype(bf16) for c in range(depth // 128)]
            found = jnp.dot(
                jnp.concatenate(picks, axis=1), table_ref[...], preferred_element_type=f32
            )
            chosen = jnp.zeros((128, cols), f32)
            for g in range(parts):
                chosen = jnp.where(rest == g, found[:, g * cols : (g + 1) * cols], chosen)
            out_ref[r * 128 : (r + 1) * 128, :] = chosen.astype(bf16)

    side_by_side = table.reshape(parts, depth, cols).transpose(1, 0, 2).reshape(depth, parts * cols)
    return pl.pallas_call(
        kernel,
        grid=(count // block,),
        in_specs=[
            pl.BlockSpec((1, block // 128, 128), lambda i: (i, 0, 0)),
            pl.BlockSpec((depth, parts * cols), lambda i: (0, 0)),
        ],
        out_specs=pl.BlockSpec((block, cols), lambda i: (i, 0)),
        out_shape=jax.ShapeDtypeStruct((count, cols), bf16),
        compiler_params=pltpu.CompilerParams(vmem_limit_bytes=24 << 20),
        cost_estimate=pl.CostEstimate(
            flops=2 * count * table_rows * cols, bytes_accessed=4 << 20, transcendentals=0
        ),
    )(ids.reshape(count // block, block // 128, 128), side_by_side)


def project(rows, w_zx, w_bc, w_dt):
    count, width = rows.shape
    channels, group_cols, heads = w_zx.shape[2], w_bc.shape[2], w_dt.shape[1]
    depth = 1024
    f32 = jnp.float32

    def kernel(rows_ref, zx_ref, bc_ref, dt_ref, z_out, x_out, bc_out, dt_out):
        @pl.when(pl.program_id(0) == 0)
        def _():
            for out in (z_out, x_out, bc_out, dt_out):
                out[...] = jnp.zeros_like(out)

        part = rows_ref[...]
        zx = zx_ref[...].reshape(depth, 2 * channels)
        z_out[...] += jnp.dot(part, zx[:, :channels], preferred_element_type=f32)
        x_out[...] += jnp.dot(part, zx[:, channels:], preferred_element_type=f32)
        bc = bc_ref[...].reshape(depth, 2 * group_cols)
        bc_out[...] += jnp.dot(part, bc, preferred_element_type=f32)
        dt_out[...] += jnp.dot(part, dt_ref[...], preferred_element_type=f32)

    widths = (channels, channels, 2 * group_cols, heads)
    return pl.pallas_call(
        kernel,
        grid=(width // depth,),
        in_specs=[
            pl.BlockSpec((count, depth), lambda i: (0, i)),
            pl.BlockSpec((depth, 2, channels), lambda i: (i, 0, 0)),
            pl.BlockSpec((depth, 2, group_cols), lambda i: (i, 0, 0)),
            pl.BlockSpec((depth, heads), lambda i: (i, 0)),
        ],
        out_specs=[pl.BlockSpec((count, n), lambda i: (0, 0)) for n in widths],
        out_shape=[jax.ShapeDtypeStruct((count, n), f32) for n in widths],
        compiler_params=pltpu.CompilerParams(vmem_limit_bytes=40 << 20),
        cost_estimate=pl.CostEstimate(
            flops=2 * count * width * sum(widths),
            bytes_accessed=2 * width * sum(widths),
            transcendentals=0,
        ),
    )(rows, w_zx, w_bc, w_dt)


def rms_scale(values, gain):
    return values * lax.rsqrt(jnp.mean(values * values, axis=-1, keepdims=True) + 1e-05) * gain


def join_stats(left_set, right_set):
    peak_left, sum_left, first_left, second_left, target_left = left_set
    peak_right, sum_right, first_right, second_right, target_right = right_set
    row_peak = jnp.maximum(peak_left, peak_right)
    shift_left = peak_left - row_peak
    shift_right = peak_right - row_peak
    weight_left = jnp.exp(shift_left)
    weight_right = jnp.exp(shift_right)
    exp_sum = weight_left * sum_left + weight_right * sum_right
    first_moment = weight_left * (first_left + shift_left * sum_left) + weight_right * (
        first_right + shift_right * sum_right
    )
    second_moment = weight_left * (
        second_left + 2.0 * shift_left * first_left + shift_left * shift_left * sum_left
    ) + weight_right * (
        second_right + 2.0 * shift_right * first_right + shift_right * shift_right * sum_right
    )
    return (row_peak, exp_sum, first_moment, second_moment, target_left + target_right)


def vocab_stats(pieces, wanted, tables):
    count = sum(piece.shape[0] for piece in pieces)
    width, columns = tables[0].shape
    tile = 256
    f32 = jnp.float32

    def kernel(*refs):
        piece_refs = refs[: len(pieces)]
        wanted_ref, *table_refs, out_ref, rows_ref, logits_ref = refs[len(pieces) :]
        start = 0
        for ref in piece_refs:
            rows_ref[start : start + ref.shape[0], :] = ref[...]
            start += ref.shape[0]
        rows = rows_ref[...]
        for place, table_ref in enumerate(table_refs):
            for j in range(columns // tile):
                at = place * columns + j * tile
                logits_ref[:, at : at + tile] = jnp.dot(
                    rows, table_ref[:, j * tile : (j + 1) * tile], preferred_element_type=f32
                )
        lane = lax.broadcasted_iota(jnp.int32, (128, 128), 1)
        column = lax.broadcasted_iota(jnp.int32, (128, columns), 1)
        for r in range(count // 128):
            logits = logits_ref[r * 128 : (r + 1) * 128, :]
            peak = jnp.max(logits, axis=1, keepdims=True)
            shifted = logits - peak
            weights = jnp.exp(shifted)
            first = weights * shifted
            target = jnp.zeros((128, 1), f32)
            for place in range(len(table_refs)):
                aim = jnp.broadcast_to(wanted_ref[place, r : r + 1, :], (128, 128)).T[:, :1]
                part = logits[:, place * columns : (place + 1) * columns]
                target += jnp.sum(jnp.where(column == aim, part, 0.0), axis=1, keepdims=True)
            stats = (
                peak,
                jnp.sum(weights, axis=1, keepdims=True),
                jnp.sum(first, axis=1, keepdims=True),
                jnp.sum(first * shifted, axis=1, keepdims=True),
                target,
            )
            table = jnp.zeros((128, 128), f32)
            for k, stat in enumerate(stats):
                table = jnp.where(lane == k, stat, table)
            out_ref[:, r * 128 : (r + 1) * 128] = table.T[:8]

    whole = pl.BlockSpec(memory_space=pltpu.VMEM)
    every = len(tables) * columns
    return pl.pallas_call(
        kernel,
        in_specs=[whole] * (len(pieces) + 1 + len(tables)),
        out_specs=whole,
        out_shape=jax.ShapeDtypeStruct((8, count), f32),
        scratch_shapes=[pltpu.VMEM((count, width), jnp.bfloat16), pltpu.VMEM((count, every), f32)],
        compiler_params=pltpu.CompilerParams(vmem_limit_bytes=24 << 20),
        cost_estimate=pl.CostEstimate(
            flops=2 * count * width * every,
            bytes_accessed=2 * count * width,
            transcendentals=count * every,
        ),
    )(*pieces, wanted, *tables)


def on_device(
    token_ids,
    targets,
    embed,
    w_zx,
    w_bc,
    w_dt,
    conv_x,
    conv_bc,
    dt_bias,
    a_log,
    d_skip,
    norm_gain,
    pre_gain,
    final_gain,
    w_out,
    lm_head,
):
    bf16, f32 = jnp.bfloat16, jnp.float32
    ctx_count = lax.axis_size("ctx")
    head_count = lax.axis_size("head")
    tok_rows = token_ids.shape[0]
    quarter = tok_rows // head_count
    model_width = pre_gain.shape[0]
    head_pos = lax.axis_index("head")
    ctx_pos = lax.axis_index("ctx")
    w_out_full = lax.all_gather(w_out, "ctx", axis=1, tiled=True)

    packed = jnp.concatenate([token_ids, targets])
    packed = jnp.broadcast_to(packed[None], (ctx_count, tok_rows + quarter))
    packed = lax.all_to_all(packed, "ctx", 0, 0, tiled=True)
    all_ids = packed[:, :tok_rows].reshape(ctx_count, head_count, quarter)
    group_targets = packed[:, tok_rows:]

    table_rows, slice_cols = embed.shape
    by_owner = jnp.roll(all_ids, -head_pos, axis=1).transpose(1, 0, 2)
    local_ids = by_owner.reshape(-1) - head_pos * table_rows
    looked = look_up(local_ids, embed)
    looked = looked.reshape(head_count, ctx_count * quarter, slice_cols)
    mine = ring_reduce([looked[k] for k in range(4)], shift_head).astype(bf16)
    mine = mine.reshape(ctx_count, quarter, slice_cols)
    own_emb = lax.all_to_all(mine, "ctx", split_axis=0, concat_axis=2, tiled=True)
    own_emb = own_emb.reshape(quarter, model_width)
    normed_own = rms_scale(own_emb.astype(f32), pre_gain).astype(bf16)
    normed_in = jnp.zeros((tok_rows, model_width), bf16)
    for ahead, block in enumerate(ring_gather(normed_own, shift_head)):
        row = ((head_pos + ahead) % head_count) * quarter
        normed_in = lax.dynamic_update_slice_in_dim(normed_in, block, row, 0)

    normed_in, lm_head = lax.optimization_barrier((normed_in, lm_head))
    vocab_own = jnp.zeros((model_width, lm_head.shape[1]), bf16)
    for ahead, block in enumerate(ring_gather(lm_head, shift_head)):
        row = ((head_pos + ahead) % head_count) * lm_head.shape[0]
        vocab_own = lax.dynamic_update_slice_in_dim(vocab_own, block, row, 0)
    vocab_other = swap_core(vocab_own)

    channels = w_zx.shape[2]
    group_cols = w_bc.shape[2]
    gate_z, proj_x, proj_bc, step_raw = project(normed_in, w_zx, w_bc, w_dt)
    mixed_in = jnp.concatenate([proj_x, proj_bc], axis=1)
    conv_taps = conv_x.shape[0]
    rim_rows = passed_along(mixed_in[tok_rows - conv_taps + 1 :], "ctx", 1)
    kernel = jnp.concatenate([conv_x, conv_bc.reshape(conv_taps, 2 * group_cols)], axis=1)
    extended = jnp.concatenate([rim_rows, mixed_in], axis=0)
    convolved = jnp.zeros_like(mixed_in)
    for offset in range(conv_taps):
        convolved = convolved + kernel[offset] * extended[offset : offset + tok_rows]
    activated = jax.nn.silu(convolved)
    heads = step_raw.shape[1]
    x_heads = activated[:, :channels].reshape(tok_rows, heads, HEAD_DIM)
    b_act = activated[:, channels : channels + group_cols]
    c_act = activated[:, channels + group_cols :]
    step_size = jax.nn.softplus(step_raw + dt_bias)
    log_rate = -jnp.exp(a_log) * step_size
    positions = jnp.arange(tok_rows)
    causal = positions[:, None] >= positions[None, :]
    log_decay = jnp.dot(causal.astype(f32), log_rate, precision=exact_prec)
    log_total = log_decay[-1]

    tail_decay = jnp.exp(log_total[None, :] - log_decay) * step_size
    end_state = jnp.einsum("sh,shp,sn->hpn", tail_decay, x_heads, b_act, precision=exact_prec)
    part_rows = heads * HEAD_DIM // ctx_count
    slices = end_state.astype(bf16).reshape(ctx_count, part_rows, STATE)
    first = log_total.astype(bf16)
    second = (log_total - first.astype(f32)).astype(bf16)
    third = (log_total - first.astype(f32) - second.astype(f32)).astype(bf16)
    totals = jnp.repeat(jnp.stack([first, second, third], axis=1), ctx_count // heads, axis=0)
    totals = jnp.broadcast_to(totals[:, :, None], (ctx_count, 3, STATE))
    totals = jnp.concatenate([totals, jnp.zeros((ctx_count, 13, STATE), bf16)], axis=1)
    message = jnp.concatenate([slices, totals], axis=1)
    arrived = lax.all_to_all(message, "ctx", 0, 0, tiled=True)
    decay_gap = log_decay.T[:, :, None] - log_decay.T[:, None, :]
    decay_mask = jnp.exp(jnp.where(causal[None], decay_gap, -jnp.inf))
    scores = jnp.einsum("tn,sn->ts", c_act, b_act, precision=exact_prec)
    mixing = scores[None] * decay_mask * step_size.T[:, None, :]
    y_local = jnp.einsum("hts,shp->thp", mixing, x_heads, precision=exact_prec)
    y_local = y_local + d_skip[None, :, None] * x_heads
    arrived, y_local = lax.optimization_barrier((arrived, y_local))
    block_logs = jnp.sum(arrived[:, part_rows : part_rows + 3, 0].astype(f32), axis=1)
    blocks = jnp.arange(ctx_count)
    earlier = blocks[:, None] > blocks[None, :]
    upto = jnp.sum(jnp.where(blocks[:, None] >= blocks[None, :], block_logs[None, :], 0.0), axis=1)
    gap = (upto - block_logs)[:, None] - upto[None, :]
    weigh = jnp.exp(jnp.where(earlier, gap, -jnp.inf))
    parts = arrived[:, :part_rows].astype(f32).reshape(ctx_count, part_rows * STATE)
    entering = jnp.dot(weigh, parts, precision=exact_prec).astype(bf16)
    entering = entering.reshape(ctx_count, part_rows, STATE)
    state_in = lax.all_to_all(entering, "ctx", 0, 0, tiled=True)
    state_in = state_in.reshape(heads, HEAD_DIM, STATE).astype(f32)

    y_carry = (
        jnp.einsum("tn,hpn->thp", c_act, state_in, precision=exact_prec)
        * jnp.exp(log_decay)[:, :, None]
    )
    mixer_out = y_local + y_carry
    gated_raw = mixer_out.reshape(tok_rows, channels) * jax.nn.silu(gate_z)
    gated_out = rms_scale(gated_raw, norm_gain).astype(bf16)

    partial_out = jnp.dot(gated_out, w_out_full, preferred_element_type=f32).astype(bf16)
    partial_out = partial_out.reshape(head_count, quarter, model_width)
    by_owner_out = jnp.roll(partial_out, -head_pos, axis=0)
    summed_out = ring_reduce([by_owner_out[k] for k in range(4)], shift_head)
    residual = (own_emb.astype(f32) + summed_out).astype(bf16)
    normed_out = rms_scale(residual.astype(f32), final_gain).astype(bf16)

    along_first, along_second = shift_mixed(True), shift_mixed(False)
    from_left = moved(normed_out, along_first, 1)
    from_right = moved(normed_out, along_first, -1)
    from_far = moved(normed_out, along_first, 2)
    near = jnp.concatenate([normed_out, from_left])
    rest = jnp.concatenate([from_right, from_far])
    near_left = moved(near, along_second, 1)
    near_right = moved(near, along_second, -1)
    rest_left = moved(rest, along_second, 1)
    rest_right = moved(rest, along_second, -1)
    near_far = moved(near_left, along_second, 1)
    rest_far = moved(rest_right, along_second, -1)
    pieces = ((near, rest), (near_right, rest_right), (near_far, rest_far), (near_left, rest_left))
    order = (0, 3, 1, 2)
    y_pos, z_pos, core = ctx_pos // 8, (ctx_pos // 2) % 4, ctx_pos % 2
    by_chip = lax.dynamic_index_in_dim(group_targets.reshape(4, 4, 2, quarter), core, 2, False)
    by_chip = jnp.roll(by_chip, (-y_pos, -z_pos), (0, 1))
    by_chip = jnp.where(core == 0, by_chip, by_chip.transpose(1, 0, 2))
    by_chip = jnp.stack([by_chip[:, k] for k in order], axis=1).reshape(4, 1, 4 * quarter)
    vocab_width = vocab_own.shape[1]
    by_chip = jnp.stack([by_chip - ctx_pos * vocab_width, by_chip - (ctx_pos ^ 1) * vocab_width])
    tables = (vocab_own, vocab_other)
    rows = 4 * quarter
    stats = [vocab_stats(pieces[0], by_chip[:, 0], tables)]
    sides = vocab_stats(pieces[1] + pieces[3], jnp.concatenate([by_chip[:, 1], by_chip[:, 3]], axis=1), tables)
    stats.append(moved(sides[:, :rows], along_second, 1))
    stats.append(moved(vocab_stats(pieces[2], by_chip[:, 2], tables), along_second, 2))
    stats.append(moved(sides[:, rows:], along_second, -1))
    merged = tuple(stats[0][:5])
    for other in (stats[1], stats[3], stats[2]):
        merged = join_stats(merged, tuple(other[:5]))
    both = jnp.stack(merged).reshape(5, 4, quarter)
    merged = tuple(both[:, 0])
    for place in range(1, 4):
        merged = join_stats(merged, tuple(moved(both[:, place], along_first, order[place])))
    row_peak, exp_sum, first_moment, second_moment, target_logit = merged
    mean_shift = first_moment / exp_sum
    spread = second_moment / exp_sum - mean_shift * mean_shift
    return (target_logit - row_peak - mean_shift) * lax.rsqrt(jnp.maximum(spread, 0.25))


def solution(mesh):
    placed = (
        P("ctx"),
        P(("ctx", "head")),
        P("head", "ctx"),
        P(None, None, "head"),
        P(None, None, "head"),
        P(None, "head"),
        P(None, "head"),
        P(None, None, "head"),
        P("head"),
        P("head"),
        P("head"),
        P("head"),
        P(),
        P(),
        P("head", "ctx"),
        P("head", "ctx"),
    )
    return jax.shard_map(
        on_device, mesh=mesh, in_specs=placed, out_specs=P(("ctx", "head")), check_vma=False
    )
```

```python
import jax
import jax.numpy as jnp
from jax import lax
from jax.experimental import pallas as pl
from jax.experimental.pallas import tpu as pltpu
from jax.sharding import PartitionSpec as P

HEAD_DIM = 64
STATE = 128


exact_prec = lax.Precision.HIGHEST


def shift_head(by):
    return "head", [(i, (i + by) % 4) for i in range(4)]


def shift_mixed(first):
    def shift(by):
        pairs = []
        for i in range(32):
            y, z, core = i // 8, (i // 2) % 4, i % 2
            if (core == 0) == first:
                z = (z + by) % 4
            else:
                y = (y + by) % 4
            pairs.append((i, y * 8 + z * 2 + core))
        return "ctx", pairs

    return shift


def swap_core(value):
    return lax.ppermute(value, "ctx", [(i, i ^ 1) for i in range(32)])


def moved(value, shift, by):
    axis, pairs = shift(by)
    return lax.ppermute(value, axis, pairs)


def passed_along(value, axis, by):
    length = lax.axis_size(axis)
    pairs = [(i, i + by) for i in range(length) if 0 <= i + by < length]
    return lax.ppermute(value, axis, pairs)


def ring_gather(value, shift):
    half = value.shape[0] // 2
    left = moved(value, shift, 1)
    right = moved(value, shift, -1)
    left, right = lax.optimization_barrier((left, right))
    far_low = moved(left[:half], shift, 1)
    far_high = moved(right[half:], shift, -1)
    return value, right, far_low, far_high, left


def ring_reduce(parts, shift):
    own, ahead, far, behind = parts
    half = own.shape[0] // 2
    from_left = moved(far[:half], shift, 1)
    from_right = moved(far[half:], shift, -1)
    from_left, from_right = lax.optimization_barrier((from_left, from_right))
    ahead = jnp.concatenate([ahead[:half] + from_left, ahead[half:]])
    behind = jnp.concatenate([behind[:half], behind[half:] + from_right])
    left = moved(ahead, shift, 1)
    right = moved(behind, shift, -1)
    f32 = jnp.float32
    return own.astype(f32) + left.astype(f32) + right.astype(f32)


def in_vmem():
    return pl.BlockSpec(memory_space=pltpu.VMEM)


def spot(index):
    group = jnp.bitwise_and(jnp.right_shift(index, 5), 3)
    return group * 128 + jnp.right_shift(index, 7) * 32 + jnp.bitwise_and(index, 31)


def pack_columns(table):
    rows = table.shape[0] // 4
    bf16, f32 = jnp.bfloat16, jnp.float32

    def kernel(table_ref, out_ref):
        row = lax.broadcasted_iota(jnp.int32, (512, 512), 0)
        col = lax.broadcasted_iota(jnp.int32, (512, 512), 1)
        swap = (col == spot(row)).astype(f32).astype(bf16)
        for at in range(0, rows, 256):
            wide = [table_ref[g * rows + at : g * rows + at + 256, :] for g in range(4)]
            wide = jnp.concatenate(wide, axis=1)
            swapped = jnp.dot(wide, swap, preferred_element_type=f32).astype(bf16)
            for h in range(4):
                out_ref[h, at : at + 256, :] = swapped[:, h * 128 : (h + 1) * 128]

    return pl.pallas_call(
        kernel,
        in_specs=[in_vmem()],
        out_specs=in_vmem(),
        out_shape=jax.ShapeDtypeStruct((4, rows, 128), bf16),
        compiler_params=pltpu.CompilerParams(vmem_limit_bytes=16 << 20),
        cost_estimate=pl.CostEstimate(
            flops=2 * rows * 512 * 512, bytes_accessed=8 * rows * 128 * 2, transcendentals=0
        ),
    )(table)


def look_up(ids, table):
    steps = ids.shape[0]
    bf16, f32 = jnp.bfloat16, jnp.float32

    def kernel(ids_ref, table_ref, out_ref, side_ref):
        @pl.when(pl.program_id(0) == 0)
        def _():
            for q in range(8):
                rows = pl.ds((q % 2) * 512, 512)
                side_ref[:, q * 128 : (q + 1) * 128] = table_ref[q // 2, rows, :]

        lane = lax.broadcasted_iota(jnp.int32, (128, 128), 1)
        row = lax.broadcasted_iota(jnp.int32, (128, 128), 0)
        lane_group = jnp.right_shift(lane, 5)
        same = jnp.bitwise_and(row, 31) == jnp.bitwise_and(lane, 31)
        total = jnp.zeros((128, 128), f32)
        for g in range(4):
            column = jnp.broadcast_to(ids_ref[0, g : g + 1, :], (128, 128)).T
            low = jnp.bitwise_and(column, 511)
            picks = [(low == lane + 128 * c).astype(f32).astype(bf16) for c in range(4)]
            picks = jnp.concatenate(picks, axis=1)
            found = jnp.dot(picks, side_ref[...], preferred_element_type=f32)
            rest = jnp.right_shift(column, 9)
            here = jnp.bitwise_and(jnp.right_shift(rest, 1), 3) == lane_group
            block = jnp.where(here, jnp.bitwise_and(rest, 25), -1)
            chosen = jnp.zeros((128, 128), f32)
            for q in range(8):
                wanted = (q // 2) * 8 + q % 2
                chosen = jnp.where(block == wanted, found[:, q * 128 : (q + 1) * 128], chosen)
            fold = jnp.logical_and(same, lane_group == g).astype(f32).astype(bf16)
            total = total + jnp.dot(chosen.astype(bf16), fold, preferred_element_type=f32)
        out_ref[...] = total.astype(bf16)

    return pl.pallas_call(
        kernel,
        grid=(steps,),
        in_specs=[
            pl.BlockSpec((1, 4, 128), lambda i: (i, 0, 0)),
            pl.BlockSpec((4, 1024, 128), lambda i: (0, 0, 0)),
        ],
        out_specs=pl.BlockSpec((128, 128), lambda i: (i, 0)),
        out_shape=jax.ShapeDtypeStruct((steps * 128, 128), bf16),
        scratch_shapes=[pltpu.VMEM((512, 1024), bf16)],
        compiler_params=pltpu.CompilerParams(vmem_limit_bytes=16 << 20),
        cost_estimate=pl.CostEstimate(
            flops=2 * steps * 512 * 512 * 1024, bytes_accessed=2 << 20, transcendentals=0
        ),
    )(ids, table)


def assemble(pieces, head, gain):
    own, right, far_low, far_high, left = pieces
    blocks, quarter = own.shape[:2]
    rows, width = blocks * quarter, blocks * 128
    bf16, f32 = jnp.bfloat16, jnp.float32

    def kernel(head_ref, own_ref, right_ref, low_ref, high_ref, left_ref, gain_ref, normed_ref, quarter_ref, emb_ref):
        head = head_ref[0]
        row = lax.broadcasted_iota(jnp.int32, (512, 512), 0)
        col = lax.broadcasted_iota(jnp.int32, (512, 512), 1)
        source = jnp.bitwise_and(jnp.right_shift(row, 7) + head, 3)
        goal = spot(source * 128 + jnp.bitwise_and(row, 127))
        swap = (col == goal).astype(f32).astype(bf16)
        for at in range(0, rows, 256):
            if at < rows // 2:
                far = low_ref[at : at + 256, :]
            else:
                far = high_ref[at - rows // 2 : at - rows // 2 + 256, :]
            here = pl.ds(at, 256)
            wide = jnp.concatenate([own_ref[here, :], right_ref[here, :], far, left_ref[here, :]], axis=1)
            swapped = jnp.dot(wide, swap, preferred_element_type=f32).astype(bf16)
            for c in range(256 // quarter):
                column = (at // quarter + c) * 128
                for q in range(4):
                    emb_ref[q * quarter : (q + 1) * quarter, column : column + 128] = swapped[
                        c * quarter : (c + 1) * quarter, q * 128 : (q + 1) * 128
                    ]
        quarter_ref[...] = emb_ref[pl.ds(pl.multiple_of(head * quarter, quarter), quarter), :]
        for q in range(4):
            values = emb_ref[q * quarter : (q + 1) * quarter, :].astype(f32)
            scale = lax.rsqrt(jnp.mean(values * values, axis=1, keepdims=True) + 1e-05)
            normed_ref[q * quarter : (q + 1) * quarter, :] = (values * scale * gain_ref[...]).astype(bf16)

    flat = [piece.reshape(-1, 128) for piece in (own, right, far_low, far_high, left)]
    return pl.pallas_call(
        kernel,
        in_specs=[pl.BlockSpec(memory_space=pltpu.SMEM)] + [in_vmem()] * 6,
        out_specs=[in_vmem()] * 2,
        out_shape=[
            jax.ShapeDtypeStruct((4 * quarter, width), bf16),
            jax.ShapeDtypeStruct((quarter, width), bf16),
        ],
        scratch_shapes=[pltpu.VMEM((4 * quarter, width), bf16)],
        compiler_params=pltpu.CompilerParams(vmem_limit_bytes=16 << 20),
        cost_estimate=pl.CostEstimate(
            flops=2 * rows * 512 * 512, bytes_accessed=4 << 20, transcendentals=0
        ),
    )(head, *flat, gain.reshape(1, width))


def project_out(gated, weights, head):
    count, depth = gated.shape
    width, tile = weights.shape[1], 1024
    quarter = count // 4

    def kernel(head_ref, gated_ref, weights_ref, out_ref):
        product = jnp.dot(gated_ref[...], weights_ref[...], preferred_element_type=jnp.float32)
        for q in range(4):
            ahead = jnp.bitwise_and(q - head_ref[0], 3)
            out_ref[ahead] = product[q * quarter : (q + 1) * quarter, :].astype(jnp.bfloat16)

    return pl.pallas_call(
        kernel,
        grid=(width // tile,),
        in_specs=[
            pl.BlockSpec(memory_space=pltpu.SMEM),
            pl.BlockSpec((count, depth), lambda i: (0, 0)),
            pl.BlockSpec((depth, tile), lambda i: (0, i)),
        ],
        out_specs=pl.BlockSpec((4, quarter, tile), lambda i: (0, 0, i)),
        out_shape=jax.ShapeDtypeStruct((4, quarter, width), jnp.bfloat16),
        compiler_params=pltpu.CompilerParams(vmem_limit_bytes=12 << 20),
        cost_estimate=pl.CostEstimate(
            flops=2 * count * depth * width, bytes_accessed=2 * depth * width, transcendentals=0
        ),
    )(head, gated, weights)


def project(rows, w_zx, w_bc, w_dt):
    count, width = rows.shape
    channels, group_cols, heads = w_zx.shape[2], w_bc.shape[2], w_dt.shape[1]
    depth = 1024
    f32 = jnp.float32

    def kernel(rows_ref, zx_ref, bc_ref, dt_ref, z_out, x_out, bc_out, dt_out):
        @pl.when(pl.program_id(0) == 0)
        def _():
            for out in (z_out, x_out, bc_out, dt_out):
                out[...] = jnp.zeros_like(out)

        part = rows_ref[...]
        zx = zx_ref[...].reshape(depth, 2 * channels)
        z_out[...] += jnp.dot(part, zx[:, :channels], preferred_element_type=f32)
        x_out[...] += jnp.dot(part, zx[:, channels:], preferred_element_type=f32)
        bc = bc_ref[...].reshape(depth, 2 * group_cols)
        bc_out[...] += jnp.dot(part, bc, preferred_element_type=f32)
        dt_out[...] += jnp.dot(part, dt_ref[...], preferred_element_type=f32)

    widths = (channels, channels, 2 * group_cols, heads)
    return pl.pallas_call(
        kernel,
        grid=(width // depth,),
        in_specs=[
            pl.BlockSpec((count, depth), lambda i: (0, i)),
            pl.BlockSpec((depth, 2, channels), lambda i: (i, 0, 0)),
            pl.BlockSpec((depth, 2, group_cols), lambda i: (i, 0, 0)),
            pl.BlockSpec((depth, heads), lambda i: (i, 0)),
        ],
        out_specs=[pl.BlockSpec((count, n), lambda i: (0, 0)) for n in widths],
        out_shape=[jax.ShapeDtypeStruct((count, n), f32) for n in widths],
        compiler_params=pltpu.CompilerParams(vmem_limit_bytes=20 << 20),
        cost_estimate=pl.CostEstimate(
            flops=2 * count * width * sum(widths),
            bytes_accessed=2 * width * sum(widths),
            transcendentals=0,
        ),
    )(rows, w_zx, w_bc, w_dt)


def rms_scale(values, gain):
    return values * lax.rsqrt(jnp.mean(values * values, axis=-1, keepdims=True) + 1e-05) * gain


def join_stats(left_set, right_set):
    peak_left, sum_left, first_left, second_left, target_left = left_set
    peak_right, sum_right, first_right, second_right, target_right = right_set
    row_peak = jnp.maximum(peak_left, peak_right)
    shift_left = peak_left - row_peak
    shift_right = peak_right - row_peak
    weight_left = jnp.exp(shift_left)
    weight_right = jnp.exp(shift_right)
    exp_sum = weight_left * sum_left + weight_right * sum_right
    first_moment = weight_left * (first_left + shift_left * sum_left) + weight_right * (
        first_right + shift_right * sum_right
    )
    second_moment = weight_left * (
        second_left + 2.0 * shift_left * first_left + shift_left * shift_left * sum_left
    ) + weight_right * (
        second_right + 2.0 * shift_right * first_right + shift_right * shift_right * sum_right
    )
    return (row_peak, exp_sum, first_moment, second_moment, target_left + target_right)


def vocab_stats(pieces, wanted, tables):
    count = sum(piece.shape[0] for piece in pieces)
    width, columns = tables[0].shape
    tile = 256
    tiles = columns // tile
    f32 = jnp.float32

    def kernel(*refs):
        piece_refs = refs[: len(pieces)]
        wanted_ref, first_ref, second_ref, out_ref, rows_ref, logits_ref = refs[len(pieces) :]
        step = pl.program_id(0)

        @pl.when(step == 0)
        def _():
            start = 0
            for ref in piece_refs:
                rows_ref[start : start + ref.shape[0], :] = ref[...]
                start += ref.shape[0]

        @pl.when(step < tiles)
        def _():
            logits_ref[step] = jnp.dot(rows_ref[...], first_ref[...], preferred_element_type=f32)

        @pl.when(step >= tiles)
        def _():
            logits_ref[step] = jnp.dot(rows_ref[...], second_ref[...], preferred_element_type=f32)

        @pl.when(step == 2 * tiles - 1)
        def _():
            lane = lax.broadcasted_iota(jnp.int32, (128, 128), 1)
            column = lax.broadcasted_iota(jnp.int32, (128, columns), 1)
            for r in range(count // 128):
                logits = [logits_ref[j, r * 128 : (r + 1) * 128, :] for j in range(2 * tiles)]
                logits = jnp.concatenate(logits, axis=1)
                peak = jnp.max(logits, axis=1, keepdims=True)
                shifted = logits - peak
                weights = jnp.exp(shifted)
                first = weights * shifted
                target = jnp.zeros((128, 1), f32)
                for place in range(2):
                    aim = jnp.broadcast_to(wanted_ref[place, r : r + 1, :], (128, 128)).T[:, :1]
                    part = logits[:, place * columns : (place + 1) * columns]
                    target += jnp.sum(jnp.where(column == aim, part, 0.0), axis=1, keepdims=True)
                stats = (
                    peak,
                    jnp.sum(weights, axis=1, keepdims=True),
                    jnp.sum(first, axis=1, keepdims=True),
                    jnp.sum(first * shifted, axis=1, keepdims=True),
                    target,
                )
                table = jnp.zeros((128, 128), f32)
                for k, stat in enumerate(stats):
                    table = jnp.where(lane == k, stat, table)
                out_ref[:, r * 128 : (r + 1) * 128] = table.T[:8]

    every = 2 * columns
    return pl.pallas_call(
        kernel,
        grid=(2 * tiles,),
        in_specs=[pl.BlockSpec(piece.shape, lambda i: (0, 0)) for piece in pieces]
        + [
            pl.BlockSpec(wanted.shape, lambda i: (0, 0, 0)),
            pl.BlockSpec((width, tile), lambda i: (0, jnp.minimum(i, tiles - 1))),
            pl.BlockSpec((width, tile), lambda i: (0, jnp.maximum(i - tiles, 0))),
        ],
        out_specs=pl.BlockSpec((8, count), lambda i: (0, 0)),
        out_shape=jax.ShapeDtypeStruct((8, count), f32),
        scratch_shapes=[
            pltpu.VMEM((count, width), jnp.bfloat16),
            pltpu.VMEM((2 * tiles, count, tile), f32),
        ],
        compiler_params=pltpu.CompilerParams(vmem_limit_bytes=20 << 20),
        cost_estimate=pl.CostEstimate(
            flops=2 * count * width * every,
            bytes_accessed=2 * width * every,
            transcendentals=count * every,
        ),
    )(*pieces, wanted, *tables)


def on_device(
    token_ids,
    targets,
    embed,
    w_zx,
    w_bc,
    w_dt,
    conv_x,
    conv_bc,
    dt_bias,
    a_log,
    d_skip,
    norm_gain,
    pre_gain,
    final_gain,
    w_out,
    lm_head,
):
    bf16, f32 = jnp.bfloat16, jnp.float32
    ctx_count = lax.axis_size("ctx")
    head_count = lax.axis_size("head")
    tok_rows = token_ids.shape[0]
    quarter = tok_rows // head_count
    model_width = pre_gain.shape[0]
    head_pos = lax.axis_index("head")
    ctx_pos = lax.axis_index("ctx")
    head_at = head_pos[None].astype(jnp.int32)
    w_out_full = lax.all_gather(w_out, "ctx", axis=1, tiled=True)
    vocab_own = lax.all_gather(lm_head, "head", axis=0, tiled=True)
    vocab_other = swap_core(vocab_own)

    packed = jnp.concatenate([token_ids, targets])
    packed = jnp.broadcast_to(packed[None], (ctx_count, tok_rows + quarter))
    packed = lax.all_to_all(packed, "ctx", 0, 0, tiled=True)
    all_ids = packed[:, :tok_rows].reshape(ctx_count // 4, 4, head_count, quarter)
    group_targets = packed[:, tok_rows:]

    columns = lax.all_to_all(pack_columns(embed), "head", 0, 0, tiled=True)
    all_ids = all_ids.transpose(0, 2, 1, 3).reshape(ctx_count // 4, head_count, 4 * quarter)
    mine = look_up(all_ids, columns).reshape(ctx_count, quarter, 128)
    mine = lax.all_to_all(mine, "ctx", 0, 0, tiled=True)
    normed_in, own_emb = assemble(ring_gather(mine, shift_head), head_at, pre_gain)

    channels = w_zx.shape[2]
    group_cols = w_bc.shape[2]
    gate_z, proj_x, proj_bc, step_raw = project(normed_in, w_zx, w_bc, w_dt)
    mixed_in = jnp.concatenate([proj_x, proj_bc], axis=1)
    conv_taps = conv_x.shape[0]
    rim_rows = passed_along(mixed_in[tok_rows - conv_taps + 1 :], "ctx", 1)
    kernel = jnp.concatenate([conv_x, conv_bc.reshape(conv_taps, 2 * group_cols)], axis=1)
    extended = jnp.concatenate([rim_rows, mixed_in], axis=0)
    convolved = jnp.zeros_like(mixed_in)
    for offset in range(conv_taps):
        convolved = convolved + kernel[offset] * extended[offset : offset + tok_rows]
    activated = jax.nn.silu(convolved)
    heads = step_raw.shape[1]
    x_heads = activated[:, :channels].reshape(tok_rows, heads, HEAD_DIM)
    b_act = activated[:, channels : channels + group_cols]
    c_act = activated[:, channels + group_cols :]
    step_size = jax.nn.softplus(step_raw + dt_bias)
    log_rate = -jnp.exp(a_log) * step_size
    positions = jnp.arange(tok_rows)
    causal = positions[:, None] >= positions[None, :]
    log_decay = jnp.dot(causal.astype(f32), log_rate, precision=exact_prec)
    log_total = log_decay[-1]

    tail_decay = jnp.exp(log_total[None, :] - log_decay) * step_size
    end_state = jnp.einsum("sh,shp,sn->hpn", tail_decay, x_heads, b_act, precision=exact_prec)
    part_rows = heads * HEAD_DIM // ctx_count
    slices = end_state.astype(bf16).reshape(ctx_count, part_rows, STATE)
    first = log_total.astype(bf16)
    second = (log_total - first.astype(f32)).astype(bf16)
    third = (log_total - first.astype(f32) - second.astype(f32)).astype(bf16)
    totals = jnp.repeat(jnp.stack([first, second, third], axis=1), ctx_count // heads, axis=0)
    totals = jnp.broadcast_to(totals[:, :, None], (ctx_count, 3, STATE))
    totals = jnp.concatenate([totals, jnp.zeros((ctx_count, 13, STATE), bf16)], axis=1)
    message = jnp.concatenate([slices, totals], axis=1)
    arrived = lax.all_to_all(message, "ctx", 0, 0, tiled=True)
    decay_gap = log_decay.T[:, :, None] - log_decay.T[:, None, :]
    decay_mask = jnp.exp(jnp.where(causal[None], decay_gap, -jnp.inf))
    scores = jnp.einsum("tn,sn->ts", c_act, b_act, precision=exact_prec)
    mixing = scores[None] * decay_mask * step_size.T[:, None, :]
    y_local = jnp.einsum("hts,shp->thp", mixing, x_heads, precision=exact_prec)
    y_local = y_local + d_skip[None, :, None] * x_heads
    arrived, y_local = lax.optimization_barrier((arrived, y_local))
    block_logs = jnp.sum(arrived[:, part_rows : part_rows + 3, 0].astype(f32), axis=1)
    blocks = jnp.arange(ctx_count)
    earlier = blocks[:, None] > blocks[None, :]
    upto = jnp.sum(jnp.where(blocks[:, None] >= blocks[None, :], block_logs[None, :], 0.0), axis=1)
    gap = (upto - block_logs)[:, None] - upto[None, :]
    weigh = jnp.exp(jnp.where(earlier, gap, -jnp.inf))
    parts = arrived[:, :part_rows].astype(f32).reshape(ctx_count, part_rows * STATE)
    entering = jnp.dot(weigh, parts, precision=exact_prec).astype(bf16)
    entering = entering.reshape(ctx_count, part_rows, STATE)
    state_in = lax.all_to_all(entering, "ctx", 0, 0, tiled=True)
    state_in = state_in.reshape(heads, HEAD_DIM, STATE).astype(f32)

    y_carry = (
        jnp.einsum("tn,hpn->thp", c_act, state_in, precision=exact_prec)
        * jnp.exp(log_decay)[:, :, None]
    )
    mixer_out = y_local + y_carry
    gated_raw = mixer_out.reshape(tok_rows, channels) * jax.nn.silu(gate_z)
    gated_out = rms_scale(gated_raw, norm_gain).astype(bf16)

    partial_out = project_out(gated_out, w_out_full, head_at)
    summed_out = ring_reduce([partial_out[k] for k in range(4)], shift_head)
    residual = (own_emb.astype(f32) + summed_out).astype(bf16)
    normed_out = rms_scale(residual.astype(f32), final_gain).astype(bf16)

    along_first, along_second = shift_mixed(True), shift_mixed(False)
    from_left = moved(normed_out, along_first, 1)
    from_right = moved(normed_out, along_first, -1)
    from_far = moved(normed_out, along_first, 2)
    near = jnp.concatenate([normed_out, from_left])
    rest = jnp.concatenate([from_right, from_far])
    near_left = moved(near, along_second, 1)
    near_right = moved(near, along_second, -1)
    rest_left = moved(rest, along_second, 1)
    rest_right = moved(rest, along_second, -1)
    y_pos, z_pos, core = ctx_pos // 8, (ctx_pos // 2) % 4, ctx_pos % 2
    by_chip = lax.dynamic_index_in_dim(group_targets.reshape(4, 4, 2, quarter), core, 2, False)
    by_chip = jnp.roll(by_chip, (-y_pos, -z_pos), (0, 1))
    by_chip = jnp.where(core == 0, by_chip, by_chip.transpose(1, 0, 2))
    order = (0, 3, 1, 2)
    by_chip = jnp.stack([by_chip[:, k] for k in order], axis=1).reshape(4, 1, 4 * quarter)
    vocab_width = vocab_own.shape[1]
    by_chip = jnp.stack([by_chip - ctx_pos * vocab_width, by_chip - (ctx_pos ^ 1) * vocab_width])
    tables = (vocab_own, vocab_other)
    rows = 4 * quarter
    stats = [vocab_stats((near, rest), by_chip[:, 0], tables)]
    near_left, rest_right, stats[0] = lax.optimization_barrier((near_left, rest_right, stats[0]))
    near_far = moved(near_left, along_second, 1)
    rest_far = moved(rest_right, along_second, -1)
    aims = jnp.concatenate([by_chip[:, 1], by_chip[:, 3]], axis=1)
    sides = vocab_stats((near_right, rest_right, near_left, rest_left), aims, tables)
    stats.append(moved(sides[:, :rows], along_second, 1))
    stats.append(moved(vocab_stats((near_far, rest_far), by_chip[:, 2], tables), along_second, 2))
    stats.append(moved(sides[:, rows:], along_second, -1))
    merged = tuple(stats[0][:5])
    for other in (stats[1], stats[3], stats[2]):
        merged = join_stats(merged, tuple(other[:5]))
    both = jnp.stack(merged).reshape(5, 4, quarter)
    merged = tuple(both[:, 0])
    for place in range(1, 4):
        merged = join_stats(merged, tuple(moved(both[:, place], along_first, order[place])))
    row_peak, exp_sum, first_moment, second_moment, target_logit = merged
    mean_shift = first_moment / exp_sum
    spread = second_moment / exp_sum - mean_shift * mean_shift
    return (target_logit - row_peak - mean_shift) * lax.rsqrt(jnp.maximum(spread, 0.25))


def solution(mesh):
    placed = (
        P("ctx"),
        P(("ctx", "head")),
        P("head", "ctx"),
        P(None, None, "head"),
        P(None, None, "head"),
        P(None, "head"),
        P(None, "head"),
        P(None, None, "head"),
        P("head"),
        P("head"),
        P("head"),
        P("head"),
        P(),
        P(),
        P("head", "ctx"),
        P("head", "ctx"),
    )
    return jax.shard_map(
        on_device, mesh=mesh, in_specs=placed, out_specs=P(("ctx", "head")), check_vma=False
    )
```

```python
import jax
import jax.numpy as jnp
from jax import lax
from jax.experimental import pallas as pl
from jax.experimental.pallas import tpu as pltpu
from jax.sharding import PartitionSpec as P

HEAD_DIM = 64
STATE = 128


exact_prec = lax.Precision.HIGHEST


def shift_head(by):
    return "head", [(i, (i + by) % 4) for i in range(4)]


def shift_mixed(first):
    def shift(by):
        pairs = []
        for i in range(32):
            y, z, core = i // 8, (i // 2) % 4, i % 2
            if (core == 0) == first:
                z = (z + by) % 4
            else:
                y = (y + by) % 4
            pairs.append((i, y * 8 + z * 2 + core))
        return "ctx", pairs

    return shift


def swap_core(value):
    return lax.ppermute(value, "ctx", [(i, i ^ 1) for i in range(32)])


def moved(value, shift, by):
    axis, pairs = shift(by)
    return lax.ppermute(value, axis, pairs)


def passed_along(value, axis, by):
    length = lax.axis_size(axis)
    pairs = [(i, i + by) for i in range(length) if 0 <= i + by < length]
    return lax.ppermute(value, axis, pairs)


def ring_gather(value, shift):
    return (value, *(moved(value, shift, -ahead) for ahead in (1, 2, 3)))


def ring_reduce(parts, shift):
    arrived = [moved(parts[ahead], shift, ahead) for ahead in (1, 2, 3)]
    total = parts[0].astype(jnp.float32)
    for part in arrived:
        total = total + part.astype(jnp.float32)
    return total


def in_vmem():
    return pl.BlockSpec(memory_space=pltpu.VMEM)


def spot(index):
    group = jnp.bitwise_and(jnp.right_shift(index, 5), 3)
    return group * 128 + jnp.right_shift(index, 7) * 32 + jnp.bitwise_and(index, 31)


def swap_matrix(head):
    row = lax.broadcasted_iota(jnp.int32, (512, 512), 0)
    col = lax.broadcasted_iota(jnp.int32, (512, 512), 1)
    source = jnp.bitwise_and(jnp.right_shift(row, 7) + head, 3)
    goal = spot(source * 128 + jnp.bitwise_and(row, 127))
    return (col == goal).astype(jnp.float32).astype(jnp.bfloat16)


def pack_columns(table, head):
    rows = table.shape[0] // 4
    bf16, f32 = jnp.bfloat16, jnp.float32

    def kernel(head_ref, table_ref, *out_refs):
        row = lax.broadcasted_iota(jnp.int32, (512, 512), 0)
        col = lax.broadcasted_iota(jnp.int32, (512, 512), 1)
        owner = jnp.bitwise_and(jnp.right_shift(row, 5), 3)
        ahead = jnp.bitwise_and(owner - head_ref[0], 3)
        goal = ahead * 128 + jnp.right_shift(row, 7) * 32 + jnp.bitwise_and(row, 31)
        swap = (col == goal).astype(f32).astype(bf16)
        for at in range(0, rows, 256):
            wide = [table_ref[g * rows + at : g * rows + at + 256, :] for g in range(4)]
            wide = jnp.concatenate(wide, axis=1)
            swapped = jnp.dot(wide, swap, preferred_element_type=f32).astype(bf16)
            for k, out_ref in enumerate(out_refs):
                out_ref[at : at + 256, :] = swapped[:, k * 128 : (k + 1) * 128]

    return pl.pallas_call(
        kernel,
        in_specs=[pl.BlockSpec(memory_space=pltpu.SMEM), in_vmem()],
        out_specs=[in_vmem()] * 4,
        out_shape=[jax.ShapeDtypeStruct((rows, 128), bf16)] * 4,
        compiler_params=pltpu.CompilerParams(vmem_limit_bytes=16 << 20),
        cost_estimate=pl.CostEstimate(
            flops=2 * rows * 512 * 512, bytes_accessed=8 * rows * 128 * 2, transcendentals=0
        ),
    )(head, table)


def look_up(ids, tables):
    steps, sets = ids.shape[0], ids.shape[1] // 4
    bf16, f32 = jnp.bfloat16, jnp.float32

    def kernel(ids_ref, *refs):
        table_refs, (out_ref, side_ref) = refs[:4], refs[4:]

        @pl.when(pl.program_id(0) == 0)
        def _():
            for q in range(8):
                rows = pl.ds((q % 2) * 512, 512)
                side_ref[:, q * 128 : (q + 1) * 128] = table_refs[q // 2][rows, :]

        lane = lax.broadcasted_iota(jnp.int32, (128, 128), 1)
        lane_group = jnp.right_shift(lane, 5)
        row = lax.broadcasted_iota(jnp.int32, (512, 128), 0)
        spread = lax.broadcasted_iota(jnp.int32, (512, 128), 1)
        goal = jnp.right_shift(row, 7) * 32 + jnp.bitwise_and(row, 31)
        fold = (spread == goal).astype(f32).astype(bf16)
        for t in range(sets):
            picked = []
            for g in range(4):
                column = jnp.broadcast_to(ids_ref[0, 4 * t + g : 4 * t + g + 1, :], (128, 128)).T
                low = jnp.bitwise_and(column, 511)
                picks = [(low == lane + 128 * c).astype(f32).astype(bf16) for c in range(4)]
                picks = jnp.concatenate(picks, axis=1)
                found = jnp.dot(picks, side_ref[...], preferred_element_type=f32)
                rest = jnp.right_shift(column, 9)
                here = jnp.bitwise_and(jnp.right_shift(rest, 1), 3) == lane_group
                block = jnp.where(here, jnp.bitwise_and(rest, 25), -1)
                chosen = jnp.zeros((128, 128), f32)
                for q in range(8):
                    wanted = (q // 2) * 8 + q % 2
                    chosen = jnp.where(block == wanted, found[:, q * 128 : (q + 1) * 128], chosen)
                picked.append(chosen.astype(bf16))
            folded = jnp.dot(jnp.concatenate(picked, axis=1), fold, preferred_element_type=f32)
            out_ref[t * 128 : (t + 1) * 128, :] = folded.astype(bf16)

    return pl.pallas_call(
        kernel,
        grid=(steps,),
        in_specs=[pl.BlockSpec((1, 4 * sets, 128), lambda i: (i, 0, 0))]
        + [pl.BlockSpec((1024, 128), lambda i: (0, 0))] * 4,
        out_specs=pl.BlockSpec((sets * 128, 128), lambda i: (i, 0)),
        out_shape=jax.ShapeDtypeStruct((steps * sets * 128, 128), bf16),
        scratch_shapes=[pltpu.VMEM((512, 1024), bf16)],
        compiler_params=pltpu.CompilerParams(vmem_limit_bytes=16 << 20),
        cost_estimate=pl.CostEstimate(
            flops=2 * steps * sets * 512 * 512 * 1024, bytes_accessed=2 << 20, transcendentals=0
        ),
    )(ids, *tables)


def embed_and_project(pieces, head, gain, w_zx, w_bc, w_dt):
    blocks, quarter = pieces[0].shape[:2]
    rows, width = blocks * quarter, blocks * 128
    count = 4 * quarter
    channels, group_cols, heads = w_zx.shape[2], w_bc.shape[2], w_dt.shape[1]
    depth = 1024
    bf16, f32 = jnp.bfloat16, jnp.float32

    def kernel(*refs):
        head_ref, piece_refs, gain_ref = refs[0], refs[1:5], refs[5]
        zx_ref, bc_ref, dt_ref, z_out, x_out, bc_out, dt_out, quarter_ref, emb_ref, normed_ref = refs[6:]
        step = pl.program_id(0)

        @pl.when(step == 0)
        def _():
            head = head_ref[0]
            swap = swap_matrix(head)
            for at in range(0, rows, 256):
                wide = jnp.concatenate([ref[at : at + 256, :] for ref in piece_refs], axis=1)
                swapped = jnp.dot(wide, swap, preferred_element_type=f32).astype(bf16)
                for c in range(256 // quarter):
                    column = (at // quarter + c) * 128
                    for q in range(4):
                        emb_ref[q * quarter : (q + 1) * quarter, column : column + 128] = swapped[
                            c * quarter : (c + 1) * quarter, q * 128 : (q + 1) * 128
                        ]
            mine = pl.ds(pl.multiple_of(head * quarter, quarter), quarter)
            quarter_ref[...] = emb_ref[mine, :]
            for q in range(4):
                at = slice(q * quarter, (q + 1) * quarter)
                values = emb_ref[at, :].astype(f32)
                scale = lax.rsqrt(jnp.mean(values * values, axis=1, keepdims=True) + 1e-05)
                values = (values * scale * gain_ref[...]).astype(bf16)
                for k in range(width // depth):
                    normed_ref[k, at, :] = values[:, k * depth : (k + 1) * depth]
            for out in (z_out, x_out, bc_out, dt_out):
                out[...] = jnp.zeros_like(out)

        part = normed_ref[step]
        zx = zx_ref[...].reshape(depth, 2 * channels)
        z_out[...] += jnp.dot(part, zx[:, :channels], preferred_element_type=f32)
        x_out[...] += jnp.dot(part, zx[:, channels:], preferred_element_type=f32)
        bc = bc_ref[...].reshape(depth, 2 * group_cols)
        bc_out[...] += jnp.dot(part, bc, preferred_element_type=f32)
        dt_out[...] += jnp.dot(part, dt_ref[...], preferred_element_type=f32)

    flat = [piece.reshape(-1, 128) for piece in pieces]
    widths = (channels, channels, 2 * group_cols, heads)
    return pl.pallas_call(
        kernel,
        grid=(width // depth,),
        in_specs=[pl.BlockSpec(memory_space=pltpu.SMEM)]
        + [pl.BlockSpec(piece.shape, lambda i: (0, 0)) for piece in flat]
        + [
            pl.BlockSpec((1, width), lambda i: (0, 0)),
            pl.BlockSpec((depth, 2, channels), lambda i: (i, 0, 0)),
            pl.BlockSpec((depth, 2, group_cols), lambda i: (i, 0, 0)),
            pl.BlockSpec((depth, heads), lambda i: (i, 0)),
        ],
        out_specs=[pl.BlockSpec((count, n), lambda i: (0, 0)) for n in widths]
        + [pl.BlockSpec((quarter, width), lambda i: (0, 0))],
        out_shape=[jax.ShapeDtypeStruct((count, n), f32) for n in widths]
        + [jax.ShapeDtypeStruct((quarter, width), bf16)],
        scratch_shapes=[
            pltpu.VMEM((count, width), bf16),
            pltpu.VMEM((width // depth, count, depth), bf16),
        ],
        compiler_params=pltpu.CompilerParams(vmem_limit_bytes=48 << 20),
        cost_estimate=pl.CostEstimate(
            flops=2 * count * width * sum(widths),
            bytes_accessed=2 * width * sum(widths),
            transcendentals=0,
        ),
    )(head, *flat, gain.reshape(1, width), w_zx, w_bc, w_dt)


def project_out(gated, weights, head):
    count, depth = gated.shape
    width, tile = weights.shape[1], 1024
    quarter = count // 4

    def kernel(head_ref, gated_ref, weights_ref, out_ref):
        product = jnp.dot(gated_ref[...], weights_ref[...], preferred_element_type=jnp.float32)
        for q in range(4):
            ahead = jnp.bitwise_and(q - head_ref[0], 3)
            out_ref[ahead] = product[q * quarter : (q + 1) * quarter, :].astype(jnp.bfloat16)

    return pl.pallas_call(
        kernel,
        grid=(width // tile,),
        in_specs=[
            pl.BlockSpec(memory_space=pltpu.SMEM),
            pl.BlockSpec((count, depth), lambda i: (0, 0)),
            pl.BlockSpec((depth, tile), lambda i: (0, i)),
        ],
        out_specs=pl.BlockSpec((4, quarter, tile), lambda i: (0, 0, i)),
        out_shape=jax.ShapeDtypeStruct((4, quarter, width), jnp.bfloat16),
        compiler_params=pltpu.CompilerParams(vmem_limit_bytes=48 << 20),
        cost_estimate=pl.CostEstimate(
            flops=2 * count * depth * width, bytes_accessed=2 * depth * width, transcendentals=0
        ),
    )(head, gated, weights)


def rms_scale(values, gain):
    return values * lax.rsqrt(jnp.mean(values * values, axis=-1, keepdims=True) + 1e-05) * gain


def join_stats(left_set, right_set):
    peak_left, sum_left, first_left, second_left, target_left = left_set
    peak_right, sum_right, first_right, second_right, target_right = right_set
    row_peak = jnp.maximum(peak_left, peak_right)
    shift_left = peak_left - row_peak
    shift_right = peak_right - row_peak
    weight_left = jnp.exp(shift_left)
    weight_right = jnp.exp(shift_right)
    exp_sum = weight_left * sum_left + weight_right * sum_right
    first_moment = weight_left * (first_left + shift_left * sum_left) + weight_right * (
        first_right + shift_right * sum_right
    )
    second_moment = weight_left * (
        second_left + 2.0 * shift_left * first_left + shift_left * shift_left * sum_left
    ) + weight_right * (
        second_right + 2.0 * shift_right * first_right + shift_right * shift_right * sum_right
    )
    return (row_peak, exp_sum, first_moment, second_moment, target_left + target_right)


def vocab_stats(pieces, wanted, tables):
    count = sum(piece.shape[0] for piece in pieces)
    width, columns = tables[0].shape
    tile = 256
    tiles = columns // tile
    f32 = jnp.float32

    def kernel(*refs):
        piece_refs = refs[: len(pieces)]
        wanted_ref, first_ref, second_ref, out_ref, rows_ref, logits_ref = refs[len(pieces) :]
        step = pl.program_id(0)

        @pl.when(step == 0)
        def _():
            start = 0
            for ref in piece_refs:
                rows_ref[start : start + ref.shape[0], :] = ref[...]
                start += ref.shape[0]

        @pl.when(step < tiles)
        def _():
            logits_ref[step] = jnp.dot(rows_ref[...], first_ref[...], preferred_element_type=f32)

        @pl.when(step >= tiles)
        def _():
            logits_ref[step] = jnp.dot(rows_ref[...], second_ref[...], preferred_element_type=f32)

        @pl.when(step == 2 * tiles - 1)
        def _():
            lane = lax.broadcasted_iota(jnp.int32, (128, 128), 1)
            column = lax.broadcasted_iota(jnp.int32, (128, columns), 1)
            for r in range(count // 128):
                logits = [logits_ref[j, r * 128 : (r + 1) * 128, :] for j in range(2 * tiles)]
                logits = jnp.concatenate(logits, axis=1)
                peak = jnp.max(logits, axis=1, keepdims=True)
                shifted = logits - peak
                weights = jnp.exp(shifted)
                first = weights * shifted
                target = jnp.zeros((128, 1), f32)
                for place in range(2):
                    aim = jnp.broadcast_to(wanted_ref[place, r : r + 1, :], (128, 128)).T[:, :1]
                    part = logits[:, place * columns : (place + 1) * columns]
                    target += jnp.sum(jnp.where(column == aim, part, 0.0), axis=1, keepdims=True)
                stats = (
                    peak,
                    jnp.sum(weights, axis=1, keepdims=True),
                    jnp.sum(first, axis=1, keepdims=True),
                    jnp.sum(first * shifted, axis=1, keepdims=True),
                    target,
                )
                table = jnp.zeros((128, 128), f32)
                for k, stat in enumerate(stats):
                    table = jnp.where(lane == k, stat, table)
                out_ref[:, r * 128 : (r + 1) * 128] = table.T[:8]

    every = 2 * columns
    return pl.pallas_call(
        kernel,
        grid=(2 * tiles,),
        in_specs=[pl.BlockSpec(piece.shape, lambda i: (0, 0)) for piece in pieces]
        + [
            pl.BlockSpec(wanted.shape, lambda i: (0, 0, 0)),
            pl.BlockSpec((width, tile), lambda i: (0, jnp.minimum(i, tiles - 1))),
            pl.BlockSpec((width, tile), lambda i: (0, jnp.maximum(i - tiles, 0))),
        ],
        out_specs=pl.BlockSpec((8, count), lambda i: (0, 0)),
        out_shape=jax.ShapeDtypeStruct((8, count), f32),
        scratch_shapes=[
            pltpu.VMEM((count, width), jnp.bfloat16),
            pltpu.VMEM((2 * tiles, count, tile), f32),
        ],
        compiler_params=pltpu.CompilerParams(vmem_limit_bytes=48 << 20),
        cost_estimate=pl.CostEstimate(
            flops=2 * count * width * every,
            bytes_accessed=2 * width * every,
            transcendentals=count * every,
        ),
    )(*pieces, wanted, *tables)


def on_device(
    token_ids,
    targets,
    embed,
    w_zx,
    w_bc,
    w_dt,
    conv_x,
    conv_bc,
    dt_bias,
    a_log,
    d_skip,
    norm_gain,
    pre_gain,
    final_gain,
    w_out,
    lm_head,
):
    bf16, f32 = jnp.bfloat16, jnp.float32
    ctx_count = lax.axis_size("ctx")
    head_count = lax.axis_size("head")
    tok_rows = token_ids.shape[0]
    quarter = tok_rows // head_count
    model_width = pre_gain.shape[0]
    head_pos = lax.axis_index("head")
    ctx_pos = lax.axis_index("ctx")
    head_at = head_pos[None].astype(jnp.int32)
    w_out_full = lax.all_gather(w_out, "ctx", axis=1, tiled=True)
    vocab_own = lax.all_gather(lm_head, "head", axis=0, tiled=True)
    vocab_other = swap_core(vocab_own)

    leaving = pack_columns(embed, head_at)
    columns = [
        leaving[0],
        moved(leaving[3], shift_head, -1),
        moved(leaving[2], shift_head, 2),
        moved(leaving[1], shift_head, 1),
    ]
    packed = jnp.concatenate([token_ids, targets])
    packed = jnp.broadcast_to(packed[None], (ctx_count, tok_rows + quarter))
    packed, leaving = lax.optimization_barrier((packed, leaving))
    packed = lax.all_to_all(packed, "ctx", 0, 0, tiled=True)
    group_targets = packed[:, tok_rows:]
    all_ids = packed[:, :tok_rows] - head_pos * embed.shape[0]
    all_ids = jnp.bitwise_and(all_ids, head_count * embed.shape[0] - 1)
    all_ids = all_ids.reshape(ctx_count // 4, 4, head_count, quarter).transpose(0, 2, 1, 3)
    mine = look_up(all_ids.reshape(2, ctx_count // 2, 4 * quarter), columns)
    mine = mine.reshape(ctx_count, quarter, 128)
    mine = lax.all_to_all(mine, "ctx", 0, 0, tiled=True)

    channels = w_zx.shape[2]
    group_cols = w_bc.shape[2]
    gate_z, proj_x, proj_bc, step_raw, own_emb = embed_and_project(
        ring_gather(mine, shift_head), head_at, pre_gain, w_zx, w_bc, w_dt
    )
    mixed_in = jnp.concatenate([proj_x, proj_bc], axis=1)
    conv_taps = conv_x.shape[0]
    rim_rows = passed_along(mixed_in[tok_rows - conv_taps + 1 :], "ctx", 1)
    kernel = jnp.concatenate([conv_x, conv_bc.reshape(conv_taps, 2 * group_cols)], axis=1)
    extended = jnp.concatenate([rim_rows, mixed_in], axis=0)
    convolved = jnp.zeros_like(mixed_in)
    for offset in range(conv_taps):
        convolved = convolved + kernel[offset] * extended[offset : offset + tok_rows]
    activated = jax.nn.silu(convolved)
    heads = step_raw.shape[1]
    x_heads = activated[:, :channels].reshape(tok_rows, heads, HEAD_DIM)
    b_act = activated[:, channels : channels + group_cols]
    c_act = activated[:, channels + group_cols :]
    step_size = jax.nn.softplus(step_raw + dt_bias)
    log_rate = -jnp.exp(a_log) * step_size
    positions = jnp.arange(tok_rows)
    causal = positions[:, None] >= positions[None, :]
    log_decay = jnp.dot(causal.astype(f32), log_rate, precision=exact_prec)
    log_total = log_decay[-1]

    tail_decay = jnp.exp(log_total[None, :] - log_decay) * step_size
    end_state = jnp.einsum("sh,shp,sn->hpn", tail_decay, x_heads, b_act, precision=exact_prec)
    part_rows = heads * HEAD_DIM // ctx_count
    slices = end_state.astype(bf16).reshape(ctx_count, part_rows, STATE)
    first = log_total.astype(bf16)
    second = (log_total - first.astype(f32)).astype(bf16)
    third = (log_total - first.astype(f32) - second.astype(f32)).astype(bf16)
    totals = jnp.repeat(jnp.stack([first, second, third], axis=1), ctx_count // heads, axis=0)
    totals = jnp.broadcast_to(totals[:, :, None], (ctx_count, 3, STATE))
    totals = jnp.concatenate([totals, jnp.zeros((ctx_count, 13, STATE), bf16)], axis=1)
    message = jnp.concatenate([slices, totals], axis=1)
    arrived = lax.all_to_all(message, "ctx", 0, 0, tiled=True)
    decay_gap = log_decay.T[:, :, None] - log_decay.T[:, None, :]
    decay_mask = jnp.exp(jnp.where(causal[None], decay_gap, -jnp.inf))
    scores = jnp.einsum("tn,sn->ts", c_act, b_act, precision=exact_prec)
    mixing = scores[None] * decay_mask * step_size.T[:, None, :]
    y_local = jnp.einsum("hts,shp->thp", mixing, x_heads, precision=exact_prec)
    y_local = y_local + d_skip[None, :, None] * x_heads
    arrived, y_local = lax.optimization_barrier((arrived, y_local))
    block_logs = jnp.sum(arrived[:, part_rows : part_rows + 3, 0].astype(f32), axis=1)
    blocks = jnp.arange(ctx_count)
    earlier = blocks[:, None] > blocks[None, :]
    upto = jnp.sum(jnp.where(blocks[:, None] >= blocks[None, :], block_logs[None, :], 0.0), axis=1)
    gap = (upto - block_logs)[:, None] - upto[None, :]
    weigh = jnp.exp(jnp.where(earlier, gap, -jnp.inf))
    parts = arrived[:, :part_rows].astype(f32).reshape(ctx_count, part_rows * STATE)
    entering = jnp.dot(weigh, parts, precision=exact_prec).astype(bf16)
    entering = entering.reshape(ctx_count, part_rows, STATE)
    state_in = lax.all_to_all(entering, "ctx", 0, 0, tiled=True)
    state_in = state_in.reshape(heads, HEAD_DIM, STATE).astype(f32)

    y_carry = (
        jnp.einsum("tn,hpn->thp", c_act, state_in, precision=exact_prec)
        * jnp.exp(log_decay)[:, :, None]
    )
    mixer_out = y_local + y_carry
    gated_raw = mixer_out.reshape(tok_rows, channels) * jax.nn.silu(gate_z)
    gated_out = rms_scale(gated_raw, norm_gain).astype(bf16)

    partial_out = project_out(gated_out, w_out_full, head_at)
    summed_out = ring_reduce([partial_out[k] for k in range(4)], shift_head)
    residual = (own_emb.astype(f32) + summed_out).astype(bf16)
    normed_out = rms_scale(residual.astype(f32), final_gain).astype(bf16)

    along_first, along_second = shift_mixed(True), shift_mixed(False)
    own, right, far, left = ring_gather(normed_out, along_first)
    near = jnp.concatenate([own, left])
    rest = jnp.concatenate([right, far])
    near_right = moved(near, along_second, -1)
    near_left = moved(near, along_second, 1)
    near_far = moved(near, along_second, 2)
    rest_right = moved(rest, along_second, -1)
    rest_left = moved(rest, along_second, 1)
    rest_far = moved(rest, along_second, 2)
    y_pos, z_pos, core = ctx_pos // 8, (ctx_pos // 2) % 4, ctx_pos % 2
    by_chip = lax.dynamic_index_in_dim(group_targets.reshape(4, 4, 2, quarter), core, 2, False)
    by_chip = jnp.roll(by_chip, (-y_pos, -z_pos), (0, 1))
    by_chip = jnp.where(core == 0, by_chip, by_chip.transpose(1, 0, 2))
    order = (0, 3, 1, 2)
    by_chip = jnp.stack([by_chip[:, k] for k in order], axis=1).reshape(4, 4 * quarter)
    vocab_width = vocab_own.shape[1]
    by_chip = jnp.stack([by_chip - ctx_pos * vocab_width, by_chip - (ctx_pos ^ 1) * vocab_width])
    tables = (vocab_own, vocab_other)
    pair = 2 * quarter

    def aims(places):
        picked = [by_chip[:, k, part * pair : (part + 1) * pair] for k, part in places]
        return jnp.concatenate(picked, axis=1).reshape(2, -1, 128)

    stats_own = vocab_stats((near, rest), aims(((0, 0), (0, 1))), tables)
    near_right, near_left, stats_own = lax.optimization_barrier((near_right, near_left, stats_own))
    stats_near = vocab_stats((near_right, near_left), aims(((1, 0), (3, 0))), tables)
    near_far, rest_right, rest_left, rest_far, stats_near = lax.optimization_barrier(
        (near_far, rest_right, rest_left, rest_far, stats_near)
    )
    stats_rest = vocab_stats(
        (near_far, rest_right, rest_left, rest_far), aims(((2, 0), (1, 1), (3, 1), (2, 1))), tables
    )
    found = (
        (stats_near[:, :pair], stats_rest[:, pair : 2 * pair]),
        (stats_rest[:, :pair], stats_rest[:, 3 * pair :]),
        (stats_near[:, pair:], stats_rest[:, 2 * pair : 3 * pair]),
    )
    stats = [stats_own]
    for k in range(1, 4):
        stats.append(moved(jnp.concatenate(found[k - 1], axis=1), along_second, k))
    merged = tuple(stats[0][:5])
    for other in stats[1:]:
        merged = join_stats(merged, tuple(other[:5]))
    both = jnp.stack(merged).reshape(5, 4, quarter)
    merged = tuple(both[:, 0])
    for place in range(1, 4):
        merged = join_stats(merged, tuple(moved(both[:, place], along_first, order[place])))
    row_peak, exp_sum, first_moment, second_moment, target_logit = merged
    mean_shift = first_moment / exp_sum
    spread = second_moment / exp_sum - mean_shift * mean_shift
    return (target_logit - row_peak - mean_shift) * lax.rsqrt(jnp.maximum(spread, 0.25))


def solution(mesh):
    placed = (
        P("ctx"),
        P(("ctx", "head")),
        P("head", "ctx"),
        P(None, None, "head"),
        P(None, None, "head"),
        P(None, "head"),
        P(None, "head"),
        P(None, None, "head"),
        P("head"),
        P("head"),
        P("head"),
        P("head"),
        P(),
        P(),
        P("head", "ctx"),
        P("head", "ctx"),
    )
    return jax.shard_map(
        on_device, mesh=mesh, in_specs=placed, out_specs=P(("ctx", "head")), check_vma=False
    )
```

```python
import jax
import jax.numpy as jnp
from jax import lax
from jax.experimental import pallas as pl
from jax.experimental.pallas import tpu as pltpu
from jax.sharding import PartitionSpec as P

HEAD_DIM = 64
STATE = 128


exact_prec = lax.Precision.HIGHEST


def shift_head(by):
    return "head", [(i, (i + by) % 4) for i in range(4)]


def shift_z(by):
    return "ctx", [(i, (i // 8) * 8 + ((i // 2 + by) % 4) * 2 + i % 2) for i in range(32)]


def shift_y(by):
    return "ctx", [(i, (i + 8 * by) % 32) for i in range(32)]


def swap_core(value):
    return lax.ppermute(value, "ctx", [(i, i ^ 1) for i in range(32)])


def moved(value, shift, by):
    axis, pairs = shift(by)
    return lax.ppermute(value, axis, pairs)


def passed_along(value, axis, by):
    length = lax.axis_size(axis)
    pairs = [(i, i + by) for i in range(length) if 0 <= i + by < length]
    return lax.ppermute(value, axis, pairs)


def ring_gather(value, shift):
    return (value, *(moved(value, shift, -ahead) for ahead in (1, 2, 3)))


def ring_reduce(parts, shift):
    arrived = [moved(parts[ahead], shift, ahead) for ahead in (1, 2, 3)]
    total = parts[0].astype(jnp.float32)
    for part in arrived:
        total = total + part.astype(jnp.float32)
    return total


def in_vmem():
    return pl.BlockSpec(memory_space=pltpu.VMEM)


def spot(index):
    group = jnp.bitwise_and(jnp.right_shift(index, 5), 3)
    return group * 128 + jnp.right_shift(index, 7) * 32 + jnp.bitwise_and(index, 31)


def swap_matrix(head):
    row = lax.broadcasted_iota(jnp.int32, (512, 512), 0)
    col = lax.broadcasted_iota(jnp.int32, (512, 512), 1)
    source = jnp.bitwise_and(jnp.right_shift(row, 7) + head, 3)
    goal = spot(source * 128 + jnp.bitwise_and(row, 127))
    return (col == goal).astype(jnp.float32).astype(jnp.bfloat16)


def pack_columns(table, head):
    rows = table.shape[0] // 4
    bf16, f32 = jnp.bfloat16, jnp.float32

    def kernel(head_ref, table_ref, *out_refs):
        row = lax.broadcasted_iota(jnp.int32, (512, 512), 0)
        col = lax.broadcasted_iota(jnp.int32, (512, 512), 1)
        owner = jnp.bitwise_and(jnp.right_shift(row, 5), 3)
        ahead = jnp.bitwise_and(owner - head_ref[0], 3)
        goal = ahead * 128 + jnp.right_shift(row, 7) * 32 + jnp.bitwise_and(row, 31)
        swap = (col == goal).astype(f32).astype(bf16)
        for at in range(0, rows, 256):
            wide = [table_ref[g * rows + at : g * rows + at + 256, :] for g in range(4)]
            wide = jnp.concatenate(wide, axis=1)
            swapped = jnp.dot(wide, swap, preferred_element_type=f32).astype(bf16)
            for k, out_ref in enumerate(out_refs):
                out_ref[at : at + 256, :] = swapped[:, k * 128 : (k + 1) * 128]

    return pl.pallas_call(
        kernel,
        in_specs=[pl.BlockSpec(memory_space=pltpu.SMEM), in_vmem()],
        out_specs=[in_vmem()] * 4,
        out_shape=[jax.ShapeDtypeStruct((rows, 128), bf16)] * 4,
        compiler_params=pltpu.CompilerParams(vmem_limit_bytes=16 << 20),
        cost_estimate=pl.CostEstimate(
            flops=2 * rows * 512 * 512, bytes_accessed=8 * rows * 128 * 2, transcendentals=0
        ),
    )(head, table)


def look_up(ids, tables):
    steps, sets = ids.shape[0], ids.shape[1] // 4
    bf16, f32 = jnp.bfloat16, jnp.float32

    def kernel(ids_ref, *refs):
        table_refs, (out_ref, side_ref) = refs[:4], refs[4:]

        @pl.when(pl.program_id(0) == 0)
        def _():
            for q in range(8):
                rows = pl.ds((q % 2) * 512, 512)
                side_ref[:, q * 128 : (q + 1) * 128] = table_refs[q // 2][rows, :]

        lane = lax.broadcasted_iota(jnp.int32, (128, 128), 1)
        lane_group = jnp.right_shift(lane, 5)
        row = lax.broadcasted_iota(jnp.int32, (512, 128), 0)
        spread = lax.broadcasted_iota(jnp.int32, (512, 128), 1)
        goal = jnp.right_shift(row, 7) * 32 + jnp.bitwise_and(row, 31)
        fold = (spread == goal).astype(f32).astype(bf16)
        for t in range(sets):
            picked = []
            for g in range(4):
                column = jnp.broadcast_to(ids_ref[0, 4 * t + g : 4 * t + g + 1, :], (128, 128)).T
                low = jnp.bitwise_and(column, 511)
                picks = [(low == lane + 128 * c).astype(f32).astype(bf16) for c in range(4)]
                picks = jnp.concatenate(picks, axis=1)
                found = jnp.dot(picks, side_ref[...], preferred_element_type=f32)
                rest = jnp.right_shift(column, 9)
                here = jnp.bitwise_and(jnp.right_shift(rest, 1), 3) == lane_group
                block = jnp.where(here, jnp.bitwise_and(rest, 25), -1)
                chosen = jnp.zeros((128, 128), f32)
                for q in range(8):
                    wanted = (q // 2) * 8 + q % 2
                    chosen = jnp.where(block == wanted, found[:, q * 128 : (q + 1) * 128], chosen)
                picked.append(chosen.astype(bf16))
            folded = jnp.dot(jnp.concatenate(picked, axis=1), fold, preferred_element_type=f32)
            out_ref[t * 128 : (t + 1) * 128, :] = folded.astype(bf16)

    return pl.pallas_call(
        kernel,
        grid=(steps,),
        in_specs=[pl.BlockSpec((1, 4 * sets, 128), lambda i: (i, 0, 0))]
        + [pl.BlockSpec((1024, 128), lambda i: (0, 0))] * 4,
        out_specs=pl.BlockSpec((sets * 128, 128), lambda i: (i, 0)),
        out_shape=jax.ShapeDtypeStruct((steps * sets * 128, 128), bf16),
        scratch_shapes=[pltpu.VMEM((512, 1024), bf16)],
        compiler_params=pltpu.CompilerParams(vmem_limit_bytes=16 << 20),
        cost_estimate=pl.CostEstimate(
            flops=2 * steps * sets * 512 * 512 * 1024, bytes_accessed=2 << 20, transcendentals=0
        ),
    )(ids, *tables)


def embed_and_project(pieces, head, gain, w_zx, w_bc, w_dt):
    blocks, quarter = pieces[0].shape[:2]
    rows, width = blocks * quarter, blocks * 128
    count = 4 * quarter
    channels, group_cols, heads = w_zx.shape[2], w_bc.shape[2], w_dt.shape[1]
    depth = 1024
    bf16, f32 = jnp.bfloat16, jnp.float32

    def kernel(*refs):
        head_ref, piece_refs, gain_ref = refs[0], refs[1:5], refs[5]
        zx_ref, bc_ref, dt_ref, z_out, x_out, bc_out, dt_out, quarter_ref, emb_ref, normed_ref = refs[6:]
        step = pl.program_id(0)

        @pl.when(step == 0)
        def _():
            head = head_ref[0]
            swap = swap_matrix(head)
            for at in range(0, rows, 256):
                wide = jnp.concatenate([ref[at : at + 256, :] for ref in piece_refs], axis=1)
                swapped = jnp.dot(wide, swap, preferred_element_type=f32).astype(bf16)
                for c in range(256 // quarter):
                    column = (at // quarter + c) * 128
                    for q in range(4):
                        emb_ref[q * quarter : (q + 1) * quarter, column : column + 128] = swapped[
                            c * quarter : (c + 1) * quarter, q * 128 : (q + 1) * 128
                        ]
            mine = pl.ds(pl.multiple_of(head * quarter, quarter), quarter)
            quarter_ref[...] = emb_ref[mine, :]
            for q in range(4):
                at = slice(q * quarter, (q + 1) * quarter)
                values = emb_ref[at, :].astype(f32)
                scale = lax.rsqrt(jnp.mean(values * values, axis=1, keepdims=True) + 1e-05)
                values = (values * scale * gain_ref[...]).astype(bf16)
                for k in range(width // depth):
                    normed_ref[k, at, :] = values[:, k * depth : (k + 1) * depth]
            for out in (z_out, x_out, bc_out, dt_out):
                out[...] = jnp.zeros_like(out)

        part = normed_ref[step]
        zx = zx_ref[...].reshape(depth, 2 * channels)
        z_out[...] += jnp.dot(part, zx[:, :channels], preferred_element_type=f32)
        x_out[...] += jnp.dot(part, zx[:, channels:], preferred_element_type=f32)
        bc = bc_ref[...].reshape(depth, 2 * group_cols)
        bc_out[...] += jnp.dot(part, bc, preferred_element_type=f32)
        dt_out[...] += jnp.dot(part, dt_ref[...], preferred_element_type=f32)

    flat = [piece.reshape(-1, 128) for piece in pieces]
    widths = (channels, channels, 2 * group_cols, heads)
    return pl.pallas_call(
        kernel,
        grid=(width // depth,),
        in_specs=[pl.BlockSpec(memory_space=pltpu.SMEM)]
        + [pl.BlockSpec(piece.shape, lambda i: (0, 0)) for piece in flat]
        + [
            pl.BlockSpec((1, width), lambda i: (0, 0)),
            pl.BlockSpec((depth, 2, channels), lambda i: (i, 0, 0)),
            pl.BlockSpec((depth, 2, group_cols), lambda i: (i, 0, 0)),
            pl.BlockSpec((depth, heads), lambda i: (i, 0)),
        ],
        out_specs=[pl.BlockSpec((count, n), lambda i: (0, 0)) for n in widths]
        + [pl.BlockSpec((quarter, width), lambda i: (0, 0))],
        out_shape=[jax.ShapeDtypeStruct((count, n), f32) for n in widths]
        + [jax.ShapeDtypeStruct((quarter, width), bf16)],
        scratch_shapes=[
            pltpu.VMEM((count, width), bf16),
            pltpu.VMEM((width // depth, count, depth), bf16),
        ],
        compiler_params=pltpu.CompilerParams(vmem_limit_bytes=48 << 20),
        cost_estimate=pl.CostEstimate(
            flops=2 * count * width * sum(widths),
            bytes_accessed=2 * width * sum(widths),
            transcendentals=0,
        ),
    )(head, *flat, gain.reshape(1, width), w_zx, w_bc, w_dt)


def project_out(gated, weights, head):
    count, depth = gated.shape
    width, tile = weights.shape[1], 1024
    quarter = count // 4

    def kernel(head_ref, gated_ref, weights_ref, out_ref):
        product = jnp.dot(gated_ref[...], weights_ref[...], preferred_element_type=jnp.float32)
        for q in range(4):
            ahead = jnp.bitwise_and(q - head_ref[0], 3)
            out_ref[ahead] = product[q * quarter : (q + 1) * quarter, :].astype(jnp.bfloat16)

    return pl.pallas_call(
        kernel,
        grid=(width // tile,),
        in_specs=[
            pl.BlockSpec(memory_space=pltpu.SMEM),
            pl.BlockSpec((count, depth), lambda i: (0, 0)),
            pl.BlockSpec((depth, tile), lambda i: (0, i)),
        ],
        out_specs=pl.BlockSpec((4, quarter, tile), lambda i: (0, 0, i)),
        out_shape=jax.ShapeDtypeStruct((4, quarter, width), jnp.bfloat16),
        compiler_params=pltpu.CompilerParams(vmem_limit_bytes=48 << 20),
        cost_estimate=pl.CostEstimate(
            flops=2 * count * depth * width, bytes_accessed=2 * depth * width, transcendentals=0
        ),
    )(head, gated, weights)


def rms_scale(values, gain):
    return values * lax.rsqrt(jnp.mean(values * values, axis=-1, keepdims=True) + 1e-05) * gain


def join_stats(left_set, right_set):
    peak_left, sum_left, first_left, second_left, target_left = left_set
    peak_right, sum_right, first_right, second_right, target_right = right_set
    row_peak = jnp.maximum(peak_left, peak_right)
    shift_left = peak_left - row_peak
    shift_right = peak_right - row_peak
    weight_left = jnp.exp(shift_left)
    weight_right = jnp.exp(shift_right)
    exp_sum = weight_left * sum_left + weight_right * sum_right
    first_moment = weight_left * (first_left + shift_left * sum_left) + weight_right * (
        first_right + shift_right * sum_right
    )
    second_moment = weight_left * (
        second_left + 2.0 * shift_left * first_left + shift_left * shift_left * sum_left
    ) + weight_right * (
        second_right + 2.0 * shift_right * first_right + shift_right * shift_right * sum_right
    )
    return (row_peak, exp_sum, first_moment, second_moment, target_left + target_right)


def vocab_stats(pieces, wanted, tables):
    count = sum(piece.shape[0] for piece in pieces)
    width, columns = tables[0].shape
    tile = 256
    tiles = columns // tile
    f32 = jnp.float32

    def kernel(*refs):
        piece_refs = refs[: len(pieces)]
        wanted_ref, first_ref, second_ref, out_ref, rows_ref, logits_ref = refs[len(pieces) :]
        step = pl.program_id(0)

        @pl.when(step == 0)
        def _():
            start = 0
            for ref in piece_refs:
                rows_ref[start : start + ref.shape[0], :] = ref[...]
                start += ref.shape[0]

        @pl.when(step < tiles)
        def _():
            logits_ref[step] = jnp.dot(rows_ref[...], first_ref[...], preferred_element_type=f32)

        @pl.when(step >= tiles)
        def _():
            logits_ref[step] = jnp.dot(rows_ref[...], second_ref[...], preferred_element_type=f32)

        @pl.when(step == 2 * tiles - 1)
        def _():
            lane = lax.broadcasted_iota(jnp.int32, (128, 128), 1)
            column = lax.broadcasted_iota(jnp.int32, (128, columns), 1)
            for r in range(count // 128):
                logits = [logits_ref[j, r * 128 : (r + 1) * 128, :] for j in range(2 * tiles)]
                logits = jnp.concatenate(logits, axis=1)
                peak = jnp.max(logits, axis=1, keepdims=True)
                shifted = logits - peak
                weights = jnp.exp(shifted)
                first = weights * shifted
                target = jnp.zeros((128, 1), f32)
                for place in range(2):
                    aim = jnp.broadcast_to(wanted_ref[place, r : r + 1, :], (128, 128)).T[:, :1]
                    part = logits[:, place * columns : (place + 1) * columns]
                    target += jnp.sum(jnp.where(column == aim, part, 0.0), axis=1, keepdims=True)
                stats = (
                    peak,
                    jnp.sum(weights, axis=1, keepdims=True),
                    jnp.sum(first, axis=1, keepdims=True),
                    jnp.sum(first * shifted, axis=1, keepdims=True),
                    target,
                )
                table = jnp.zeros((128, 128), f32)
                for k, stat in enumerate(stats):
                    table = jnp.where(lane == k, stat, table)
                out_ref[:, r * 128 : (r + 1) * 128] = table.T[:8]

    every = 2 * columns
    return pl.pallas_call(
        kernel,
        grid=(2 * tiles,),
        in_specs=[pl.BlockSpec(piece.shape, lambda i: (0, 0)) for piece in pieces]
        + [
            pl.BlockSpec(wanted.shape, lambda i: (0, 0, 0)),
            pl.BlockSpec((width, tile), lambda i: (0, jnp.minimum(i, tiles - 1))),
            pl.BlockSpec((width, tile), lambda i: (0, jnp.maximum(i - tiles, 0))),
        ],
        out_specs=pl.BlockSpec((8, count), lambda i: (0, 0)),
        out_shape=jax.ShapeDtypeStruct((8, count), f32),
        scratch_shapes=[
            pltpu.VMEM((count, width), jnp.bfloat16),
            pltpu.VMEM((2 * tiles, count, tile), f32),
        ],
        compiler_params=pltpu.CompilerParams(vmem_limit_bytes=48 << 20),
        cost_estimate=pl.CostEstimate(
            flops=2 * count * width * every,
            bytes_accessed=2 * width * every,
            transcendentals=count * every,
        ),
    )(*pieces, wanted, *tables)


def on_device(
    token_ids,
    targets,
    embed,
    w_zx,
    w_bc,
    w_dt,
    conv_x,
    conv_bc,
    dt_bias,
    a_log,
    d_skip,
    norm_gain,
    pre_gain,
    final_gain,
    w_out,
    lm_head,
):
    bf16, f32 = jnp.bfloat16, jnp.float32
    ctx_count = lax.axis_size("ctx")
    head_count = lax.axis_size("head")
    tok_rows = token_ids.shape[0]
    quarter = tok_rows // head_count
    model_width = pre_gain.shape[0]
    head_pos = lax.axis_index("head")
    ctx_pos = lax.axis_index("ctx")
    head_at = head_pos[None].astype(jnp.int32)
    w_out_full = lax.all_gather(w_out, "ctx", axis=1, tiled=True)
    leaving = pack_columns(embed, head_at)
    columns = [
        leaving[0],
        moved(leaving[3], shift_head, -1),
        moved(leaving[2], shift_head, 2),
        moved(leaving[1], shift_head, 1),
    ]
    packed = jnp.concatenate([token_ids, targets])
    packed = jnp.broadcast_to(packed[None], (ctx_count, tok_rows + quarter))
    packed, leaving = lax.optimization_barrier((packed, leaving))
    packed = lax.all_to_all(packed, "ctx", 0, 0, tiled=True)
    packed, lm_head = lax.optimization_barrier((packed, lm_head))
    vocab_own = lax.all_gather(lm_head, "head", axis=0, tiled=True)
    vocab_other = swap_core(vocab_own)
    group_targets = packed[:, tok_rows:]
    all_ids = packed[:, :tok_rows] - head_pos * embed.shape[0]
    all_ids = jnp.bitwise_and(all_ids, head_count * embed.shape[0] - 1)
    all_ids = all_ids.reshape(ctx_count // 4, 4, head_count, quarter).transpose(0, 2, 1, 3)
    mine = look_up(all_ids.reshape(2, ctx_count // 2, 4 * quarter), columns)
    mine = mine.reshape(ctx_count, quarter, 128)
    mine = lax.all_to_all(mine, "ctx", 0, 0, tiled=True)

    channels = w_zx.shape[2]
    group_cols = w_bc.shape[2]
    gate_z, proj_x, proj_bc, step_raw, own_emb = embed_and_project(
        ring_gather(mine, shift_head), head_at, pre_gain, w_zx, w_bc, w_dt
    )
    mixed_in = jnp.concatenate([proj_x, proj_bc], axis=1)
    conv_taps = conv_x.shape[0]
    rim_rows = passed_along(mixed_in[tok_rows - conv_taps + 1 :], "ctx", 1)
    kernel = jnp.concatenate([conv_x, conv_bc.reshape(conv_taps, 2 * group_cols)], axis=1)
    extended = jnp.concatenate([rim_rows, mixed_in], axis=0)
    convolved = jnp.zeros_like(mixed_in)
    for offset in range(conv_taps):
        convolved = convolved + kernel[offset] * extended[offset : offset + tok_rows]
    activated = jax.nn.silu(convolved)
    heads = step_raw.shape[1]
    x_heads = activated[:, :channels].reshape(tok_rows, heads, HEAD_DIM)
    b_act = activated[:, channels : channels + group_cols]
    c_act = activated[:, channels + group_cols :]
    step_size = jax.nn.softplus(step_raw + dt_bias)
    log_rate = -jnp.exp(a_log) * step_size
    positions = jnp.arange(tok_rows)
    causal = positions[:, None] >= positions[None, :]
    log_decay = jnp.dot(causal.astype(f32), log_rate, precision=exact_prec)
    log_total = log_decay[-1]

    tail_decay = jnp.exp(log_total[None, :] - log_decay) * step_size
    end_state = jnp.einsum("sh,shp,sn->hpn", tail_decay, x_heads, b_act, precision=exact_prec)
    part_rows = heads * HEAD_DIM // ctx_count
    slices = end_state.astype(bf16).reshape(ctx_count, part_rows, STATE)
    first = log_total.astype(bf16)
    second = (log_total - first.astype(f32)).astype(bf16)
    third = (log_total - first.astype(f32) - second.astype(f32)).astype(bf16)
    totals = jnp.repeat(jnp.stack([first, second, third], axis=1), ctx_count // heads, axis=0)
    totals = jnp.broadcast_to(totals[:, :, None], (ctx_count, 3, STATE))
    totals = jnp.concatenate([totals, jnp.zeros((ctx_count, 13, STATE), bf16)], axis=1)
    message = jnp.concatenate([slices, totals], axis=1)
    arrived = lax.all_to_all(message, "ctx", 0, 0, tiled=True)
    decay_gap = log_decay.T[:, :, None] - log_decay.T[:, None, :]
    decay_mask = jnp.exp(jnp.where(causal[None], decay_gap, -jnp.inf))
    scores = jnp.einsum("tn,sn->ts", c_act, b_act, precision=exact_prec)
    mixing = scores[None] * decay_mask * step_size.T[:, None, :]
    y_local = jnp.einsum("hts,shp->thp", mixing, x_heads, precision=exact_prec)
    y_local = y_local + d_skip[None, :, None] * x_heads
    arrived, y_local = lax.optimization_barrier((arrived, y_local))
    block_logs = jnp.sum(arrived[:, part_rows : part_rows + 3, 0].astype(f32), axis=1)
    blocks = jnp.arange(ctx_count)
    earlier = blocks[:, None] > blocks[None, :]
    upto = jnp.sum(jnp.where(blocks[:, None] >= blocks[None, :], block_logs[None, :], 0.0), axis=1)
    gap = (upto - block_logs)[:, None] - upto[None, :]
    weigh = jnp.exp(jnp.where(earlier, gap, -jnp.inf))
    parts = arrived[:, :part_rows].astype(f32).reshape(ctx_count, part_rows * STATE)
    entering = jnp.dot(weigh, parts, precision=exact_prec).astype(bf16)
    entering = entering.reshape(ctx_count, part_rows, STATE)
    state_in = lax.all_to_all(entering, "ctx", 0, 0, tiled=True)
    state_in = state_in.reshape(heads, HEAD_DIM, STATE).astype(f32)

    y_carry = (
        jnp.einsum("tn,hpn->thp", c_act, state_in, precision=exact_prec)
        * jnp.exp(log_decay)[:, :, None]
    )
    mixer_out = y_local + y_carry
    gated_raw = mixer_out.reshape(tok_rows, channels) * jax.nn.silu(gate_z)
    gated_out = rms_scale(gated_raw, norm_gain).astype(bf16)

    partial_out = project_out(gated_out, w_out_full, head_at)
    summed_out = ring_reduce([partial_out[k] for k in range(4)], shift_head)
    residual = (own_emb.astype(f32) + summed_out).astype(bf16)
    normed_out = rms_scale(residual.astype(f32), final_gain).astype(bf16)

    half = quarter // 2
    over_z = jnp.concatenate(ring_gather(normed_out[:half], shift_z))
    over_y = jnp.concatenate(ring_gather(normed_out[half:], shift_y))
    low = {ahead: moved(over_z, shift_y, -ahead) for ahead in (1, 3, 2)}
    high = {ahead: moved(over_y, shift_z, -ahead) for ahead in (1, 3, 2)}

    y_pos, z_pos, core = ctx_pos // 8, (ctx_pos // 2) % 4, ctx_pos % 2
    by_chip = lax.dynamic_index_in_dim(group_targets.reshape(4, 4, 2, quarter), core, 2, False)
    by_chip = jnp.roll(by_chip, (-y_pos, -z_pos), (0, 1))
    vocab_width = vocab_own.shape[1]
    by_chip = jnp.stack([by_chip - ctx_pos * vocab_width, by_chip - (ctx_pos ^ 1) * vocab_width])
    tables = (vocab_own, vocab_other)
    piece = 4 * half

    def aims(places):
        picked = [by_chip[:, k, :, :half].reshape(2, piece) for k in places]
        picked += [by_chip[:, :, k, half:].reshape(2, piece) for k in places]
        return jnp.concatenate(picked, axis=1).reshape(2, -1, 128)

    stats = [None] * 4
    own = vocab_stats((over_z, over_y), aims((0,)), tables)
    stats[0] = (own[:, :piece], own[:, piece:])
    low[1], low[3], high[1], high[3], own = lax.optimization_barrier((low[1], low[3], high[1], high[3], own))
    near = vocab_stats((low[1], low[3], high[1], high[3]), aims((1, 3)), tables)
    low[2], high[2], near = lax.optimization_barrier((low[2], high[2], near))
    near = [near[:, k * piece : (k + 1) * piece] for k in range(4)]
    stats[1], stats[3] = (near[0], near[2]), (near[1], near[3])
    far = vocab_stats((low[2], high[2]), aims((2,)), tables)
    stats[2] = (far[:, :piece], far[:, piece:])
    low_stats = jnp.stack([pair[0][:5].reshape(5, 4, half) for pair in stats], axis=1)
    high_stats = jnp.stack([pair[1][:5].reshape(5, 4, half) for pair in stats], axis=2)
    both = jnp.concatenate([low_stats, high_stats], axis=3).reshape(5, 4, 4 * quarter)
    merged = tuple(both[:, 0])
    for ahead in range(1, 4):
        merged = join_stats(merged, tuple(moved(both[:, ahead], shift_y, ahead)))
    both = jnp.stack(merged).reshape(5, 4, quarter)
    merged = tuple(both[:, 0])
    for ahead in range(1, 4):
        merged = join_stats(merged, tuple(moved(both[:, ahead], shift_z, ahead)))
    row_peak, exp_sum, first_moment, second_moment, target_logit = merged
    mean_shift = first_moment / exp_sum
    spread = second_moment / exp_sum - mean_shift * mean_shift
    return (target_logit - row_peak - mean_shift) * lax.rsqrt(jnp.maximum(spread, 0.25))


def solution(mesh):
    placed = (
        P("ctx"),
        P(("ctx", "head")),
        P("head", "ctx"),
        P(None, None, "head"),
        P(None, None, "head"),
        P(None, "head"),
        P(None, "head"),
        P(None, None, "head"),
        P("head"),
        P("head"),
        P("head"),
        P("head"),
        P(),
        P(),
        P("head", "ctx"),
        P("head", "ctx"),
    )
    return jax.shard_map(
        on_device, mesh=mesh, in_specs=placed, out_specs=P(("ctx", "head")), check_vma=False
    )
```

```python
import jax
import jax.numpy as jnp
from jax import lax
from jax.experimental import pallas as pl
from jax.experimental.pallas import tpu as pltpu
from jax.sharding import PartitionSpec as P

HEAD_DIM = 64
STATE = 128


exact_prec = lax.Precision.HIGHEST


def shift_head(by):
    return "head", [(i, (i + by) % 4) for i in range(4)]


def shift_mixed(first):
    def shift(by):
        pairs = []
        for i in range(32):
            y, z, core = i // 8, (i // 2) % 4, i % 2
            if (core == 0) == first:
                z = (z + by) % 4
            else:
                y = (y + by) % 4
            pairs.append((i, y * 8 + z * 2 + core))
        return "ctx", pairs

    return shift


def swap_core(value):
    return lax.ppermute(value, "ctx", [(i, i ^ 1) for i in range(32)])


def moved(value, shift, by):
    axis, pairs = shift(by)
    return lax.ppermute(value, axis, pairs)


def passed_along(value, axis, by):
    length = lax.axis_size(axis)
    pairs = [(i, i + by) for i in range(length) if 0 <= i + by < length]
    return lax.ppermute(value, axis, pairs)


def ring_gather(value, shift):
    return (value, *(moved(value, shift, -ahead) for ahead in (1, 2, 3)))


def ring_reduce(parts, shift):
    arrived = [moved(parts[ahead], shift, ahead) for ahead in (1, 2, 3)]
    total = parts[0].astype(jnp.float32)
    for part in arrived:
        total = total + part.astype(jnp.float32)
    return total


def in_vmem():
    return pl.BlockSpec(memory_space=pltpu.VMEM)


def spot(index):
    group = jnp.bitwise_and(jnp.right_shift(index, 5), 3)
    return group * 128 + jnp.right_shift(index, 7) * 32 + jnp.bitwise_and(index, 31)


def swap_matrix(head):
    row = lax.broadcasted_iota(jnp.int32, (512, 512), 0)
    col = lax.broadcasted_iota(jnp.int32, (512, 512), 1)
    source = jnp.bitwise_and(jnp.right_shift(row, 7) + head, 3)
    goal = spot(source * 128 + jnp.bitwise_and(row, 127))
    return (col == goal).astype(jnp.float32).astype(jnp.bfloat16)


def pack_columns(table, head):
    rows = table.shape[0] // 4
    bf16, f32 = jnp.bfloat16, jnp.float32

    def kernel(head_ref, table_ref, *out_refs):
        row = lax.broadcasted_iota(jnp.int32, (512, 512), 0)
        col = lax.broadcasted_iota(jnp.int32, (512, 512), 1)
        owner = jnp.bitwise_and(jnp.right_shift(row, 5), 3)
        ahead = jnp.bitwise_and(owner - head_ref[0], 3)
        goal = ahead * 128 + jnp.right_shift(row, 7) * 32 + jnp.bitwise_and(row, 31)
        swap = (col == goal).astype(f32).astype(bf16)
        for at in range(0, rows, 256):
            wide = [table_ref[g * rows + at : g * rows + at + 256, :] for g in range(4)]
            wide = jnp.concatenate(wide, axis=1)
            swapped = jnp.dot(wide, swap, preferred_element_type=f32).astype(bf16)
            for k, out_ref in enumerate(out_refs):
                out_ref[at : at + 256, :] = swapped[:, k * 128 : (k + 1) * 128]

    return pl.pallas_call(
        kernel,
        in_specs=[pl.BlockSpec(memory_space=pltpu.SMEM), in_vmem()],
        out_specs=[in_vmem()] * 4,
        out_shape=[jax.ShapeDtypeStruct((rows, 128), bf16)] * 4,
        compiler_params=pltpu.CompilerParams(vmem_limit_bytes=16 << 20),
        cost_estimate=pl.CostEstimate(
            flops=2 * rows * 512 * 512, bytes_accessed=8 * rows * 128 * 2, transcendentals=0
        ),
    )(head, table)


def look_up(ids, tables):
    steps, sets = ids.shape[0], ids.shape[1] // 4
    bf16, f32 = jnp.bfloat16, jnp.float32

    def kernel(ids_ref, *refs):
        table_refs, (out_ref, side_ref) = refs[:4], refs[4:]

        @pl.when(pl.program_id(0) == 0)
        def _():
            for q in range(8):
                rows = pl.ds((q % 2) * 512, 512)
                side_ref[:, q * 128 : (q + 1) * 128] = table_refs[q // 2][rows, :]

        lane = lax.broadcasted_iota(jnp.int32, (128, 128), 1)
        lane_group = jnp.right_shift(lane, 5)
        row = lax.broadcasted_iota(jnp.int32, (512, 128), 0)
        spread = lax.broadcasted_iota(jnp.int32, (512, 128), 1)
        goal = jnp.right_shift(row, 7) * 32 + jnp.bitwise_and(row, 31)
        fold = (spread == goal).astype(f32).astype(bf16)
        for t in range(sets):
            picked = []
            for g in range(4):
                column = jnp.broadcast_to(ids_ref[0, 4 * t + g : 4 * t + g + 1, :], (128, 128)).T
                low = jnp.bitwise_and(column, 511)
                picks = [(low == lane + 128 * c).astype(f32).astype(bf16) for c in range(4)]
                picks = jnp.concatenate(picks, axis=1)
                found = jnp.dot(picks, side_ref[...], preferred_element_type=f32)
                rest = jnp.right_shift(column, 9)
                here = jnp.bitwise_and(jnp.right_shift(rest, 1), 3) == lane_group
                block = jnp.where(here, jnp.bitwise_and(rest, 25), -1)
                chosen = jnp.zeros((128, 128), f32)
                for q in range(8):
                    wanted = (q // 2) * 8 + q % 2
                    chosen = jnp.where(block == wanted, found[:, q * 128 : (q + 1) * 128], chosen)
                picked.append(chosen.astype(bf16))
            folded = jnp.dot(jnp.concatenate(picked, axis=1), fold, preferred_element_type=f32)
            out_ref[t * 128 : (t + 1) * 128, :] = folded.astype(bf16)

    return pl.pallas_call(
        kernel,
        grid=(steps,),
        in_specs=[pl.BlockSpec((1, 4 * sets, 128), lambda i: (i, 0, 0))]
        + [pl.BlockSpec((1024, 128), lambda i: (0, 0))] * 4,
        out_specs=pl.BlockSpec((sets * 128, 128), lambda i: (i, 0)),
        out_shape=jax.ShapeDtypeStruct((steps * sets * 128, 128), bf16),
        scratch_shapes=[pltpu.VMEM((512, 1024), bf16)],
        compiler_params=pltpu.CompilerParams(vmem_limit_bytes=16 << 20),
        cost_estimate=pl.CostEstimate(
            flops=2 * steps * sets * 512 * 512 * 1024, bytes_accessed=2 << 20, transcendentals=0
        ),
    )(ids, *tables)


def embed_and_project(pieces, head, gain, w_zx, w_bc, w_dt):
    blocks, quarter = pieces[0].shape[:2]
    rows, width = blocks * quarter, blocks * 128
    count = 4 * quarter
    channels, group_cols, heads = w_zx.shape[2], w_bc.shape[2], w_dt.shape[1]
    depth = 1024
    bf16, f32 = jnp.bfloat16, jnp.float32

    def kernel(*refs):
        head_ref, piece_refs, gain_ref = refs[0], refs[1:5], refs[5]
        zx_ref, bc_ref, dt_ref, z_out, x_out, bc_out, dt_out, quarter_ref, emb_ref, normed_ref = refs[6:]
        step = pl.program_id(0)

        @pl.when(step == 0)
        def _():
            head = head_ref[0]
            swap = swap_matrix(head)
            for at in range(0, rows, 256):
                wide = jnp.concatenate([ref[at : at + 256, :] for ref in piece_refs], axis=1)
                swapped = jnp.dot(wide, swap, preferred_element_type=f32).astype(bf16)
                for c in range(256 // quarter):
                    column = (at // quarter + c) * 128
                    for q in range(4):
                        emb_ref[q * quarter : (q + 1) * quarter, column : column + 128] = swapped[
                            c * quarter : (c + 1) * quarter, q * 128 : (q + 1) * 128
                        ]
            mine = pl.ds(pl.multiple_of(head * quarter, quarter), quarter)
            quarter_ref[...] = emb_ref[mine, :]
            for q in range(4):
                at = slice(q * quarter, (q + 1) * quarter)
                values = emb_ref[at, :].astype(f32)
                scale = lax.rsqrt(jnp.mean(values * values, axis=1, keepdims=True) + 1e-05)
                values = (values * scale * gain_ref[...]).astype(bf16)
                for k in range(width // depth):
                    normed_ref[k, at, :] = values[:, k * depth : (k + 1) * depth]
            for out in (z_out, x_out, bc_out, dt_out):
                out[...] = jnp.zeros_like(out)

        part = normed_ref[step]
        zx = zx_ref[...].reshape(depth, 2 * channels)
        z_out[...] += jnp.dot(part, zx[:, :channels], preferred_element_type=f32)
        x_out[...] += jnp.dot(part, zx[:, channels:], preferred_element_type=f32)
        bc = bc_ref[...].reshape(depth, 2 * group_cols)
        bc_out[...] += jnp.dot(part, bc, preferred_element_type=f32)
        dt_out[...] += jnp.dot(part, dt_ref[...], preferred_element_type=f32)

    flat = [piece.reshape(-1, 128) for piece in pieces]
    widths = (channels, channels, 2 * group_cols, heads)
    return pl.pallas_call(
        kernel,
        grid=(width // depth,),
        in_specs=[pl.BlockSpec(memory_space=pltpu.SMEM)]
        + [pl.BlockSpec(piece.shape, lambda i: (0, 0)) for piece in flat]
        + [
            pl.BlockSpec((1, width), lambda i: (0, 0)),
            pl.BlockSpec((depth, 2, channels), lambda i: (i, 0, 0)),
            pl.BlockSpec((depth, 2, group_cols), lambda i: (i, 0, 0)),
            pl.BlockSpec((depth, heads), lambda i: (i, 0)),
        ],
        out_specs=[pl.BlockSpec((count, n), lambda i: (0, 0)) for n in widths]
        + [pl.BlockSpec((quarter, width), lambda i: (0, 0))],
        out_shape=[jax.ShapeDtypeStruct((count, n), f32) for n in widths]
        + [jax.ShapeDtypeStruct((quarter, width), bf16)],
        scratch_shapes=[
            pltpu.VMEM((count, width), bf16),
            pltpu.VMEM((width // depth, count, depth), bf16),
        ],
        compiler_params=pltpu.CompilerParams(vmem_limit_bytes=48 << 20),
        cost_estimate=pl.CostEstimate(
            flops=2 * count * width * sum(widths),
            bytes_accessed=2 * width * sum(widths),
            transcendentals=0,
        ),
    )(head, *flat, gain.reshape(1, width), w_zx, w_bc, w_dt)


def project_out(gated, weights, head):
    count, depth = gated.shape
    width, tile = weights.shape[1], 1024
    quarter = count // 4

    def kernel(head_ref, gated_ref, weights_ref, out_ref):
        product = jnp.dot(gated_ref[...], weights_ref[...], preferred_element_type=jnp.float32)
        for q in range(4):
            ahead = jnp.bitwise_and(q - head_ref[0], 3)
            out_ref[ahead] = product[q * quarter : (q + 1) * quarter, :].astype(jnp.bfloat16)

    return pl.pallas_call(
        kernel,
        grid=(width // tile,),
        in_specs=[
            pl.BlockSpec(memory_space=pltpu.SMEM),
            pl.BlockSpec((count, depth), lambda i: (0, 0)),
            pl.BlockSpec((depth, tile), lambda i: (0, i)),
        ],
        out_specs=pl.BlockSpec((4, quarter, tile), lambda i: (0, 0, i)),
        out_shape=jax.ShapeDtypeStruct((4, quarter, width), jnp.bfloat16),
        compiler_params=pltpu.CompilerParams(vmem_limit_bytes=48 << 20),
        cost_estimate=pl.CostEstimate(
            flops=2 * count * depth * width, bytes_accessed=2 * depth * width, transcendentals=0
        ),
    )(head, gated, weights)


def rms_scale(values, gain):
    return values * lax.rsqrt(jnp.mean(values * values, axis=-1, keepdims=True) + 1e-05) * gain


def join_stats(left_set, right_set):
    peak_left, sum_left, first_left, second_left, target_left = left_set
    peak_right, sum_right, first_right, second_right, target_right = right_set
    row_peak = jnp.maximum(peak_left, peak_right)
    shift_left = peak_left - row_peak
    shift_right = peak_right - row_peak
    weight_left = jnp.exp(shift_left)
    weight_right = jnp.exp(shift_right)
    exp_sum = weight_left * sum_left + weight_right * sum_right
    first_moment = weight_left * (first_left + shift_left * sum_left) + weight_right * (
        first_right + shift_right * sum_right
    )
    second_moment = weight_left * (
        second_left + 2.0 * shift_left * first_left + shift_left * shift_left * sum_left
    ) + weight_right * (
        second_right + 2.0 * shift_right * first_right + shift_right * shift_right * sum_right
    )
    return (row_peak, exp_sum, first_moment, second_moment, target_left + target_right)


def vocab_stats(pieces, wanted, tables):
    count = sum(piece.shape[0] for piece in pieces)
    width, columns = tables[0].shape
    tile = 256
    tiles = columns // tile
    f32 = jnp.float32

    def kernel(*refs):
        piece_refs = refs[: len(pieces)]
        wanted_ref, first_ref, second_ref, out_ref, rows_ref, logits_ref = refs[len(pieces) :]
        step = pl.program_id(0)

        @pl.when(step == 0)
        def _():
            start = 0
            for ref in piece_refs:
                rows_ref[start : start + ref.shape[0], :] = ref[...]
                start += ref.shape[0]

        @pl.when(step < tiles)
        def _():
            logits_ref[step] = jnp.dot(rows_ref[...], first_ref[...], preferred_element_type=f32)

        @pl.when(step >= tiles)
        def _():
            logits_ref[step] = jnp.dot(rows_ref[...], second_ref[...], preferred_element_type=f32)

        @pl.when(step == 2 * tiles - 1)
        def _():
            lane = lax.broadcasted_iota(jnp.int32, (128, 128), 1)
            column = lax.broadcasted_iota(jnp.int32, (128, columns), 1)
            for r in range(count // 128):
                logits = [logits_ref[j, r * 128 : (r + 1) * 128, :] for j in range(2 * tiles)]
                logits = jnp.concatenate(logits, axis=1)
                peak = jnp.max(logits, axis=1, keepdims=True)
                shifted = logits - peak
                weights = jnp.exp(shifted)
                first = weights * shifted
                target = jnp.zeros((128, 1), f32)
                for place in range(2):
                    aim = jnp.broadcast_to(wanted_ref[place, r : r + 1, :], (128, 128)).T[:, :1]
                    part = logits[:, place * columns : (place + 1) * columns]
                    target += jnp.sum(jnp.where(column == aim, part, 0.0), axis=1, keepdims=True)
                stats = (
                    peak,
                    jnp.sum(weights, axis=1, keepdims=True),
                    jnp.sum(first, axis=1, keepdims=True),
                    jnp.sum(first * shifted, axis=1, keepdims=True),
                    target,
                )
                table = jnp.zeros((128, 128), f32)
                for k, stat in enumerate(stats):
                    table = jnp.where(lane == k, stat, table)
                out_ref[:, r * 128 : (r + 1) * 128] = table.T[:8]

    every = 2 * columns
    return pl.pallas_call(
        kernel,
        grid=(2 * tiles,),
        in_specs=[pl.BlockSpec(piece.shape, lambda i: (0, 0)) for piece in pieces]
        + [
            pl.BlockSpec(wanted.shape, lambda i: (0, 0, 0)),
            pl.BlockSpec((width, tile), lambda i: (0, jnp.minimum(i, tiles - 1))),
            pl.BlockSpec((width, tile), lambda i: (0, jnp.maximum(i - tiles, 0))),
        ],
        out_specs=pl.BlockSpec((8, count), lambda i: (0, 0)),
        out_shape=jax.ShapeDtypeStruct((8, count), f32),
        scratch_shapes=[
            pltpu.VMEM((count, width), jnp.bfloat16),
            pltpu.VMEM((2 * tiles, count, tile), f32),
        ],
        compiler_params=pltpu.CompilerParams(vmem_limit_bytes=50 << 20),
        cost_estimate=pl.CostEstimate(
            flops=2 * count * width * every,
            bytes_accessed=2 * width * every,
            transcendentals=count * every,
        ),
    )(*pieces, wanted, *tables)


def on_device(
    token_ids,
    targets,
    embed,
    w_zx,
    w_bc,
    w_dt,
    conv_x,
    conv_bc,
    dt_bias,
    a_log,
    d_skip,
    norm_gain,
    pre_gain,
    final_gain,
    w_out,
    lm_head,
):
    bf16, f32 = jnp.bfloat16, jnp.float32
    ctx_count = lax.axis_size("ctx")
    head_count = lax.axis_size("head")
    tok_rows = token_ids.shape[0]
    quarter = tok_rows // head_count
    model_width = pre_gain.shape[0]
    head_pos = lax.axis_index("head")
    ctx_pos = lax.axis_index("ctx")
    head_at = head_pos[None].astype(jnp.int32)
    w_out_full = lax.all_gather(w_out, "ctx", axis=1, tiled=True)
    leaving = pack_columns(embed, head_at)
    columns = [
        leaving[0],
        moved(leaving[3], shift_head, -1),
        moved(leaving[2], shift_head, 2),
        moved(leaving[1], shift_head, 1),
    ]
    packed = jnp.concatenate([token_ids, targets])
    packed = jnp.broadcast_to(packed[None], (ctx_count, tok_rows + quarter))
    packed, leaving = lax.optimization_barrier((packed, leaving))
    packed = lax.all_to_all(packed, "ctx", 0, 0, tiled=True)
    group_targets = packed[:, tok_rows:]
    all_ids = packed[:, :tok_rows] - head_pos * embed.shape[0]
    all_ids = jnp.bitwise_and(all_ids, head_count * embed.shape[0] - 1)
    all_ids = all_ids.reshape(ctx_count // 4, 4, head_count, quarter).transpose(0, 2, 1, 3)
    mine = look_up(all_ids.reshape(2, ctx_count // 2, 4 * quarter), columns)
    mine = mine.reshape(ctx_count, quarter, 128)
    mine = lax.all_to_all(mine, "ctx", 0, 0, tiled=True)
    mine, lm_head = lax.optimization_barrier((mine, lm_head))
    vocab_own = lax.all_gather(lm_head, "head", axis=0, tiled=True)

    channels = w_zx.shape[2]
    group_cols = w_bc.shape[2]
    gate_z, proj_x, proj_bc, step_raw, own_emb = embed_and_project(
        ring_gather(mine, shift_head), head_at, pre_gain, w_zx, w_bc, w_dt
    )
    mixed_in = jnp.concatenate([proj_x, proj_bc], axis=1)
    conv_taps = conv_x.shape[0]
    rim_rows = passed_along(mixed_in[tok_rows - conv_taps + 1 :], "ctx", 1)
    kernel = jnp.concatenate([conv_x, conv_bc.reshape(conv_taps, 2 * group_cols)], axis=1)
    extended = jnp.concatenate([rim_rows, mixed_in], axis=0)
    convolved = jnp.zeros_like(mixed_in)
    for offset in range(conv_taps):
        convolved = convolved + kernel[offset] * extended[offset : offset + tok_rows]
    activated = jax.nn.silu(convolved)
    heads = step_raw.shape[1]
    x_heads = activated[:, :channels].reshape(tok_rows, heads, HEAD_DIM)
    b_act = activated[:, channels : channels + group_cols]
    c_act = activated[:, channels + group_cols :]
    step_size = jax.nn.softplus(step_raw + dt_bias)
    log_rate = -jnp.exp(a_log) * step_size
    positions = jnp.arange(tok_rows)
    causal = positions[:, None] >= positions[None, :]
    log_decay = jnp.dot(causal.astype(f32), log_rate, precision=exact_prec)
    log_total = log_decay[-1]

    tail_decay = jnp.exp(log_total[None, :] - log_decay) * step_size
    end_state = jnp.einsum("sh,shp,sn->hpn", tail_decay, x_heads, b_act, precision=exact_prec)
    part_rows = heads * HEAD_DIM // ctx_count
    slices = end_state.astype(bf16).reshape(ctx_count, part_rows, STATE)
    first = log_total.astype(bf16)
    second = (log_total - first.astype(f32)).astype(bf16)
    third = (log_total - first.astype(f32) - second.astype(f32)).astype(bf16)
    totals = jnp.repeat(jnp.stack([first, second, third], axis=1), ctx_count // heads, axis=0)
    totals = jnp.broadcast_to(totals[:, :, None], (ctx_count, 3, STATE))
    totals = jnp.concatenate([totals, jnp.zeros((ctx_count, 13, STATE), bf16)], axis=1)
    message = jnp.concatenate([slices, totals], axis=1)
    arrived = lax.all_to_all(message, "ctx", 0, 0, tiled=True)
    decay_gap = log_decay.T[:, :, None] - log_decay.T[:, None, :]
    decay_mask = jnp.exp(jnp.where(causal[None], decay_gap, -jnp.inf))
    scores = jnp.einsum("tn,sn->ts", c_act, b_act, precision=exact_prec)
    mixing = scores[None] * decay_mask * step_size.T[:, None, :]
    y_local = jnp.einsum("hts,shp->thp", mixing, x_heads, precision=exact_prec)
    y_local = y_local + d_skip[None, :, None] * x_heads
    arrived, y_local, w_out_full = lax.optimization_barrier((arrived, y_local, w_out_full))
    block_logs = jnp.sum(arrived[:, part_rows : part_rows + 3, 0].astype(f32), axis=1)
    blocks = jnp.arange(ctx_count)
    earlier = blocks[:, None] > blocks[None, :]
    upto = jnp.sum(jnp.where(blocks[:, None] >= blocks[None, :], block_logs[None, :], 0.0), axis=1)
    gap = (upto - block_logs)[:, None] - upto[None, :]
    weigh = jnp.exp(jnp.where(earlier, gap, -jnp.inf))
    parts = arrived[:, :part_rows].astype(f32).reshape(ctx_count, part_rows * STATE)
    entering = jnp.dot(weigh, parts, precision=exact_prec).astype(bf16)
    entering = entering.reshape(ctx_count, part_rows, STATE)
    state_in = lax.all_to_all(entering, "ctx", 0, 0, tiled=True)
    state_in = state_in.reshape(heads, HEAD_DIM, STATE).astype(f32)

    y_carry = (
        jnp.einsum("tn,hpn->thp", c_act, state_in, precision=exact_prec)
        * jnp.exp(log_decay)[:, :, None]
    )
    mixer_out = y_local + y_carry
    gated_raw = mixer_out.reshape(tok_rows, channels) * jax.nn.silu(gate_z)
    gated_out = rms_scale(gated_raw, norm_gain).astype(bf16)

    partial_out = project_out(gated_out, w_out_full, head_at)
    summed_out = ring_reduce([partial_out[k] for k in range(4)], shift_head)
    residual = (own_emb.astype(f32) + summed_out).astype(bf16)
    residual, vocab_own = lax.optimization_barrier((residual, vocab_own))
    vocab_other = swap_core(vocab_own)
    normed_out = rms_scale(residual.astype(f32), final_gain).astype(bf16)

    along_first, along_second = shift_mixed(True), shift_mixed(False)
    from_left = moved(normed_out, along_first, 1)
    from_right = moved(normed_out, along_first, -1)
    from_far = moved(normed_out, along_first, 2)
    near = jnp.concatenate([normed_out, from_left])
    rest = jnp.concatenate([from_right, from_far])
    near_left = moved(near, along_second, 1)
    near_right = moved(near, along_second, -1)
    rest_left = moved(rest, along_second, 1)
    rest_right = moved(rest, along_second, -1)
    y_pos, z_pos, core = ctx_pos // 8, (ctx_pos // 2) % 4, ctx_pos % 2
    by_chip = lax.dynamic_index_in_dim(group_targets.reshape(4, 4, 2, quarter), core, 2, False)
    by_chip = jnp.roll(by_chip, (-y_pos, -z_pos), (0, 1))
    by_chip = jnp.where(core == 0, by_chip, by_chip.transpose(1, 0, 2))
    order = (0, 3, 1, 2)
    by_chip = jnp.stack([by_chip[:, k] for k in order], axis=1).reshape(4, 1, 4 * quarter)
    vocab_width = vocab_own.shape[1]
    by_chip = jnp.stack([by_chip - ctx_pos * vocab_width, by_chip - (ctx_pos ^ 1) * vocab_width])
    tables = (vocab_own, vocab_other)
    rows = 4 * quarter
    near, near_left, rest_right = lax.optimization_barrier((near, near_left, rest_right))
    near_far = moved(near_left, along_second, 1)
    rest_far = moved(rest_right, along_second, -1)
    aims = jnp.concatenate([by_chip[:, k] for k in (0, 1, 3)], axis=1)
    first = (near, rest, near_right, rest_right, near_left, rest_left)
    first = vocab_stats(first, aims, tables)
    near_far, rest_far, first = lax.optimization_barrier((near_far, rest_far, first))
    last = vocab_stats((near_far, rest_far), by_chip[:, 2], tables)
    stats = [first[:, :rows]]
    stats.append(moved(first[:, rows : 2 * rows], along_second, 1))
    stats.append(moved(first[:, 2 * rows :], along_second, 3))
    stats.append(moved(last, along_second, 2))
    merged = tuple(stats[0][:5])
    for other in stats[1:]:
        merged = join_stats(merged, tuple(other[:5]))
    both = jnp.stack(merged).reshape(5, 4, quarter)
    merged = tuple(both[:, 0])
    for place in range(1, 4):
        merged = join_stats(merged, tuple(moved(both[:, place], along_first, order[place])))
    row_peak, exp_sum, first_moment, second_moment, target_logit = merged
    mean_shift = first_moment / exp_sum
    spread = second_moment / exp_sum - mean_shift * mean_shift
    return (target_logit - row_peak - mean_shift) * lax.rsqrt(jnp.maximum(spread, 0.25))


def solution(mesh):
    placed = (
        P("ctx"),
        P(("ctx", "head")),
        P("head", "ctx"),
        P(None, None, "head"),
        P(None, None, "head"),
        P(None, "head"),
        P(None, "head"),
        P(None, None, "head"),
        P("head"),
        P("head"),
        P("head"),
        P("head"),
        P(),
        P(),
        P("head", "ctx"),
        P("head", "ctx"),
    )
    return jax.shard_map(
        on_device, mesh=mesh, in_specs=placed, out_specs=P(("ctx", "head")), check_vma=False
    )
```

```python
import jax
import jax.numpy as jnp
from jax import lax
from jax.experimental import pallas as pl
from jax.experimental.pallas import tpu as pltpu
from jax.sharding import PartitionSpec as P

HEAD_DIM = 64
STATE = 128


exact_prec = lax.Precision.HIGHEST


def shift_head(by):
    return "head", [(i, (i + by) % 4) for i in range(4)]


def shift_mixed(first):
    def shift(by):
        pairs = []
        for i in range(32):
            y, z, core = i // 8, (i // 2) % 4, i % 2
            if (core == 0) == first:
                z = (z + by) % 4
            else:
                y = (y + by) % 4
            pairs.append((i, y * 8 + z * 2 + core))
        return "ctx", pairs

    return shift


def swap_core(value):
    return lax.ppermute(value, "ctx", [(i, i ^ 1) for i in range(32)])


def moved(value, shift, by):
    axis, pairs = shift(by)
    return lax.ppermute(value, axis, pairs)


def passed_along(value, axis, by):
    length = lax.axis_size(axis)
    pairs = [(i, i + by) for i in range(length) if 0 <= i + by < length]
    return lax.ppermute(value, axis, pairs)


def ring_gather(value, shift):
    return (value, *(moved(value, shift, -ahead) for ahead in (1, 2, 3)))


def ring_reduce(parts, shift):
    arrived = [moved(parts[ahead], shift, ahead) for ahead in (1, 2, 3)]
    total = parts[0].astype(jnp.float32)
    for part in arrived:
        total = total + part.astype(jnp.float32)
    return total


def in_vmem():
    return pl.BlockSpec(memory_space=pltpu.VMEM)


def spot(index):
    group = jnp.bitwise_and(jnp.right_shift(index, 5), 3)
    return group * 128 + jnp.right_shift(index, 7) * 32 + jnp.bitwise_and(index, 31)


def swap_matrix(head):
    row = lax.broadcasted_iota(jnp.int32, (512, 512), 0)
    col = lax.broadcasted_iota(jnp.int32, (512, 512), 1)
    source = jnp.bitwise_and(jnp.right_shift(row, 7) + head, 3)
    goal = spot(source * 128 + jnp.bitwise_and(row, 127))
    return (col == goal).astype(jnp.float32).astype(jnp.bfloat16)


def pack_columns(table, head):
    rows = table.shape[0] // 4
    bf16, f32 = jnp.bfloat16, jnp.float32

    def kernel(head_ref, table_ref, *out_refs):
        row = lax.broadcasted_iota(jnp.int32, (512, 512), 0)
        col = lax.broadcasted_iota(jnp.int32, (512, 512), 1)
        owner = jnp.bitwise_and(jnp.right_shift(row, 5), 3)
        ahead = jnp.bitwise_and(owner - head_ref[0], 3)
        goal = ahead * 128 + jnp.right_shift(row, 7) * 32 + jnp.bitwise_and(row, 31)
        swap = (col == goal).astype(f32).astype(bf16)
        for at in range(0, rows, 256):
            wide = [table_ref[g * rows + at : g * rows + at + 256, :] for g in range(4)]
            wide = jnp.concatenate(wide, axis=1)
            swapped = jnp.dot(wide, swap, preferred_element_type=f32).astype(bf16)
            for k, out_ref in enumerate(out_refs):
                out_ref[at : at + 256, :] = swapped[:, k * 128 : (k + 1) * 128]

    return pl.pallas_call(
        kernel,
        in_specs=[pl.BlockSpec(memory_space=pltpu.SMEM), in_vmem()],
        out_specs=[in_vmem()] * 4,
        out_shape=[jax.ShapeDtypeStruct((rows, 128), bf16)] * 4,
        compiler_params=pltpu.CompilerParams(vmem_limit_bytes=16 << 20),
        cost_estimate=pl.CostEstimate(
            flops=2 * rows * 512 * 512, bytes_accessed=8 * rows * 128 * 2, transcendentals=0
        ),
    )(head, table)


def look_up(ids, tables):
    steps, sets = ids.shape[0], ids.shape[1] // 4
    bf16, f32 = jnp.bfloat16, jnp.float32

    def kernel(ids_ref, *refs):
        table_refs, (out_ref, side_ref) = refs[:4], refs[4:]

        @pl.when(pl.program_id(0) == 0)
        def _():
            for q in range(8):
                rows = pl.ds((q % 2) * 512, 512)
                side_ref[:, q * 128 : (q + 1) * 128] = table_refs[q // 2][rows, :]

        lane = lax.broadcasted_iota(jnp.int32, (128, 128), 1)
        lane_group = jnp.right_shift(lane, 5)
        row = lax.broadcasted_iota(jnp.int32, (512, 128), 0)
        spread = lax.broadcasted_iota(jnp.int32, (512, 128), 1)
        goal = jnp.right_shift(row, 7) * 32 + jnp.bitwise_and(row, 31)
        fold = (spread == goal).astype(f32).astype(bf16)
        for t in range(sets):
            picked = []
            for g in range(4):
                column = jnp.broadcast_to(ids_ref[0, 4 * t + g : 4 * t + g + 1, :], (128, 128)).T
                low = jnp.bitwise_and(column, 511)
                picks = [(low == lane + 128 * c).astype(f32).astype(bf16) for c in range(4)]
                picks = jnp.concatenate(picks, axis=1)
                found = jnp.dot(picks, side_ref[...], preferred_element_type=f32)
                rest = jnp.right_shift(column, 9)
                here = jnp.bitwise_and(jnp.right_shift(rest, 1), 3) == lane_group
                block = jnp.where(here, jnp.bitwise_and(rest, 25), -1)
                chosen = jnp.zeros((128, 128), f32)
                for q in range(8):
                    wanted = (q // 2) * 8 + q % 2
                    chosen = jnp.where(block == wanted, found[:, q * 128 : (q + 1) * 128], chosen)
                picked.append(chosen.astype(bf16))
            folded = jnp.dot(jnp.concatenate(picked, axis=1), fold, preferred_element_type=f32)
            out_ref[t * 128 : (t + 1) * 128, :] = folded.astype(bf16)

    return pl.pallas_call(
        kernel,
        grid=(steps,),
        in_specs=[pl.BlockSpec((1, 4 * sets, 128), lambda i: (i, 0, 0))]
        + [pl.BlockSpec((1024, 128), lambda i: (0, 0))] * 4,
        out_specs=pl.BlockSpec((sets * 128, 128), lambda i: (i, 0)),
        out_shape=jax.ShapeDtypeStruct((steps * sets * 128, 128), bf16),
        scratch_shapes=[pltpu.VMEM((512, 1024), bf16)],
        compiler_params=pltpu.CompilerParams(vmem_limit_bytes=16 << 20),
        cost_estimate=pl.CostEstimate(
            flops=2 * steps * sets * 512 * 512 * 1024, bytes_accessed=2 << 20, transcendentals=0
        ),
    )(ids, *tables)


def embed_and_project(pieces, head, gain, w_zx, w_bc, w_dt):
    blocks, quarter = pieces[0].shape[:2]
    rows, width = blocks * quarter, blocks * 128
    count = 4 * quarter
    channels, group_cols, heads = w_zx.shape[2], w_bc.shape[2], w_dt.shape[1]
    depth = 1024
    bf16, f32 = jnp.bfloat16, jnp.float32

    def kernel(*refs):
        head_ref, piece_refs, gain_ref = refs[0], refs[1:5], refs[5]
        zx_ref, bc_ref, dt_ref, z_out, x_out, bc_out, dt_out, quarter_ref, emb_ref, normed_ref = refs[6:]
        step = pl.program_id(0)

        @pl.when(step == 0)
        def _():
            head = head_ref[0]
            swap = swap_matrix(head)
            for at in range(0, rows, 256):
                wide = jnp.concatenate([ref[at : at + 256, :] for ref in piece_refs], axis=1)
                swapped = jnp.dot(wide, swap, preferred_element_type=f32).astype(bf16)
                for c in range(256 // quarter):
                    column = (at // quarter + c) * 128
                    for q in range(4):
                        emb_ref[q * quarter : (q + 1) * quarter, column : column + 128] = swapped[
                            c * quarter : (c + 1) * quarter, q * 128 : (q + 1) * 128
                        ]
            mine = pl.ds(pl.multiple_of(head * quarter, quarter), quarter)
            quarter_ref[...] = emb_ref[mine, :]
            for q in range(4):
                at = slice(q * quarter, (q + 1) * quarter)
                values = emb_ref[at, :].astype(f32)
                scale = lax.rsqrt(jnp.mean(values * values, axis=1, keepdims=True) + 1e-05)
                values = (values * scale * gain_ref[...]).astype(bf16)
                for k in range(width // depth):
                    normed_ref[k, at, :] = values[:, k * depth : (k + 1) * depth]
            for out in (z_out, x_out, bc_out, dt_out):
                out[...] = jnp.zeros_like(out)

        part = normed_ref[step]
        zx = zx_ref[...].reshape(depth, 2 * channels)
        z_out[...] += jnp.dot(part, zx[:, :channels], preferred_element_type=f32)
        x_out[...] += jnp.dot(part, zx[:, channels:], preferred_element_type=f32)
        bc = bc_ref[...].reshape(depth, 2 * group_cols)
        bc_out[...] += jnp.dot(part, bc, preferred_element_type=f32)
        dt_out[...] += jnp.dot(part, dt_ref[...], preferred_element_type=f32)

    flat = [piece.reshape(-1, 128) for piece in pieces]
    widths = (channels, channels, 2 * group_cols, heads)
    return pl.pallas_call(
        kernel,
        grid=(width // depth,),
        in_specs=[pl.BlockSpec(memory_space=pltpu.SMEM)]
        + [pl.BlockSpec(piece.shape, lambda i: (0, 0)) for piece in flat]
        + [
            pl.BlockSpec((1, width), lambda i: (0, 0)),
            pl.BlockSpec((depth, 2, channels), lambda i: (i, 0, 0)),
            pl.BlockSpec((depth, 2, group_cols), lambda i: (i, 0, 0)),
            pl.BlockSpec((depth, heads), lambda i: (i, 0)),
        ],
        out_specs=[pl.BlockSpec((count, n), lambda i: (0, 0)) for n in widths]
        + [pl.BlockSpec((quarter, width), lambda i: (0, 0))],
        out_shape=[jax.ShapeDtypeStruct((count, n), f32) for n in widths]
        + [jax.ShapeDtypeStruct((quarter, width), bf16)],
        scratch_shapes=[
            pltpu.VMEM((count, width), bf16),
            pltpu.VMEM((width // depth, count, depth), bf16),
        ],
        compiler_params=pltpu.CompilerParams(vmem_limit_bytes=48 << 20),
        cost_estimate=pl.CostEstimate(
            flops=2 * count * width * sum(widths),
            bytes_accessed=2 * width * sum(widths),
            transcendentals=0,
        ),
    )(head, *flat, gain.reshape(1, width), w_zx, w_bc, w_dt)


def project_out(gated, weights, head):
    count, width = gated.shape[0], weights.shape[1]
    quarter, depth = count // 4, 256
    steps = gated.shape[1] // depth

    def kernel(head_ref, gated_ref, weights_ref, out_ref, total_ref):
        step = pl.program_id(0)
        product = jnp.dot(gated_ref[...], weights_ref[...], preferred_element_type=jnp.float32)

        @pl.when(step == 0)
        def _():
            total_ref[...] = product

        @pl.when(jnp.logical_and(step > 0, step < steps - 1))
        def _():
            total_ref[...] += product

        @pl.when(step == steps - 1)
        def _():
            total = total_ref[...] + product
            for q in range(4):
                ahead = jnp.bitwise_and(q - head_ref[0], 3)
                out_ref[ahead] = total[q * quarter : (q + 1) * quarter, :].astype(jnp.bfloat16)

    return pl.pallas_call(
        kernel,
        grid=(steps,),
        in_specs=[
            pl.BlockSpec(memory_space=pltpu.SMEM),
            pl.BlockSpec((count, depth), lambda i: (0, i)),
            pl.BlockSpec((depth, width), lambda i: (i, 0)),
        ],
        out_specs=pl.BlockSpec((4, quarter, width), lambda i: (0, 0, 0)),
        out_shape=jax.ShapeDtypeStruct((4, quarter, width), jnp.bfloat16),
        scratch_shapes=[pltpu.VMEM((count, width), jnp.float32)],
        compiler_params=pltpu.CompilerParams(vmem_limit_bytes=48 << 20),
        cost_estimate=pl.CostEstimate(
            flops=2 * count * steps * depth * width,
            bytes_accessed=2 * steps * depth * width,
            transcendentals=0,
        ),
    )(head, gated, weights)


def rms_scale(values, gain):
    return values * lax.rsqrt(jnp.mean(values * values, axis=-1, keepdims=True) + 1e-05) * gain


def join_stats(left_set, right_set):
    peak_left, sum_left, first_left, second_left, target_left = left_set
    peak_right, sum_right, first_right, second_right, target_right = right_set
    row_peak = jnp.maximum(peak_left, peak_right)
    shift_left = peak_left - row_peak
    shift_right = peak_right - row_peak
    weight_left = jnp.exp(shift_left)
    weight_right = jnp.exp(shift_right)
    exp_sum = weight_left * sum_left + weight_right * sum_right
    first_moment = weight_left * (first_left + shift_left * sum_left) + weight_right * (
        first_right + shift_right * sum_right
    )
    second_moment = weight_left * (
        second_left + 2.0 * shift_left * first_left + shift_left * shift_left * sum_left
    ) + weight_right * (
        second_right + 2.0 * shift_right * first_right + shift_right * shift_right * sum_right
    )
    return (row_peak, exp_sum, first_moment, second_moment, target_left + target_right)


def vocab_stats(pieces, wanted, tables):
    count = sum(piece.shape[0] for piece in pieces)
    width, columns = tables[0].shape
    depth = 2048
    blocks = width // depth
    f32 = jnp.float32

    def kernel(*refs):
        piece_refs = refs[: len(pieces)]
        wanted_ref, first_ref, second_ref, out_ref, rows_ref, logits_ref = refs[len(pieces) :]
        step = pl.program_id(0)

        @pl.when(step == 0)
        def _():
            start = 0
            for ref in piece_refs:
                for k in range(blocks):
                    rows_ref[k, start : start + ref.shape[0], :] = ref[:, k * depth : (k + 1) * depth]
                start += ref.shape[0]

        for place, table_ref in enumerate((first_ref, second_ref)):
            for k in range(blocks):

                @pl.when(step == place * blocks + k)
                def _(place=place, k=k, table_ref=table_ref):
                    part = jnp.dot(rows_ref[k], table_ref[...], preferred_element_type=f32)
                    if k:
                        part = part + logits_ref[place]
                    logits_ref[place] = part

        @pl.when(step == 2 * blocks - 1)
        def _():
            lane = lax.broadcasted_iota(jnp.int32, (128, 128), 1)
            column = lax.broadcasted_iota(jnp.int32, (128, columns), 1)
            for r in range(count // 128):
                logits = [logits_ref[j, r * 128 : (r + 1) * 128, :] for j in range(2)]
                logits = jnp.concatenate(logits, axis=1)
                peak = jnp.max(logits, axis=1, keepdims=True)
                shifted = logits - peak
                weights = jnp.exp(shifted)
                first = weights * shifted
                target = jnp.zeros((128, 1), f32)
                for place in range(2):
                    aim = jnp.broadcast_to(wanted_ref[place, r : r + 1, :], (128, 128)).T[:, :1]
                    part = logits[:, place * columns : (place + 1) * columns]
                    target += jnp.sum(jnp.where(column == aim, part, 0.0), axis=1, keepdims=True)
                stats = (
                    peak,
                    jnp.sum(weights, axis=1, keepdims=True),
                    jnp.sum(first, axis=1, keepdims=True),
                    jnp.sum(first * shifted, axis=1, keepdims=True),
                    target,
                )
                table = jnp.zeros((128, 128), f32)
                for k, stat in enumerate(stats):
                    table = jnp.where(lane == k, stat, table)
                out_ref[:, r * 128 : (r + 1) * 128] = table.T[:8]

    every = 2 * columns
    return pl.pallas_call(
        kernel,
        grid=(2 * blocks,),
        in_specs=[pl.BlockSpec(piece.shape, lambda i: (0, 0)) for piece in pieces]
        + [
            pl.BlockSpec(wanted.shape, lambda i: (0, 0, 0)),
            pl.BlockSpec((depth, columns), lambda i: (jnp.minimum(i, blocks - 1), 0)),
            pl.BlockSpec((depth, columns), lambda i: (jnp.maximum(i - blocks, 0), 0)),
        ],
        out_specs=pl.BlockSpec((8, count), lambda i: (0, 0)),
        out_shape=jax.ShapeDtypeStruct((8, count), f32),
        scratch_shapes=[
            pltpu.VMEM((blocks, count, depth), jnp.bfloat16),
            pltpu.VMEM((2, count, columns), f32),
        ],
        compiler_params=pltpu.CompilerParams(vmem_limit_bytes=48 << 20),
        cost_estimate=pl.CostEstimate(
            flops=2 * count * width * every,
            bytes_accessed=2 * width * every,
            transcendentals=count * every,
        ),
    )(*pieces, wanted, *tables)


def on_device(
    token_ids,
    targets,
    embed,
    w_zx,
    w_bc,
    w_dt,
    conv_x,
    conv_bc,
    dt_bias,
    a_log,
    d_skip,
    norm_gain,
    pre_gain,
    final_gain,
    w_out,
    lm_head,
):
    bf16, f32 = jnp.bfloat16, jnp.float32
    ctx_count = lax.axis_size("ctx")
    head_count = lax.axis_size("head")
    tok_rows = token_ids.shape[0]
    quarter = tok_rows // head_count
    model_width = pre_gain.shape[0]
    head_pos = lax.axis_index("head")
    ctx_pos = lax.axis_index("ctx")
    head_at = head_pos[None].astype(jnp.int32)
    w_out_full = lax.all_gather(w_out, "ctx", axis=1, tiled=True)
    leaving = pack_columns(embed, head_at)
    columns = [
        leaving[0],
        moved(leaving[3], shift_head, -1),
        moved(leaving[2], shift_head, 2),
        moved(leaving[1], shift_head, 1),
    ]
    packed = jnp.concatenate([token_ids, targets])
    packed = jnp.broadcast_to(packed[None], (ctx_count, tok_rows + quarter))
    packed, leaving = lax.optimization_barrier((packed, leaving))
    packed = lax.all_to_all(packed, "ctx", 0, 0, tiled=True)
    group_targets = packed[:, tok_rows:]
    all_ids = packed[:, :tok_rows] - head_pos * embed.shape[0]
    all_ids = jnp.bitwise_and(all_ids, head_count * embed.shape[0] - 1)
    all_ids = all_ids.reshape(ctx_count // 4, 4, head_count, quarter).transpose(0, 2, 1, 3)
    mine = look_up(all_ids.reshape(2, ctx_count // 2, 4 * quarter), columns)
    mine = mine.reshape(ctx_count, quarter, 128)
    mine = lax.all_to_all(mine, "ctx", 0, 0, tiled=True)
    mine, lm_head = lax.optimization_barrier((mine, lm_head))
    vocab_own = lax.all_gather(lm_head, "head", axis=0, tiled=True)

    channels = w_zx.shape[2]
    group_cols = w_bc.shape[2]
    gate_z, proj_x, proj_bc, step_raw, own_emb = embed_and_project(
        ring_gather(mine, shift_head), head_at, pre_gain, w_zx, w_bc, w_dt
    )
    mixed_in = jnp.concatenate([proj_x, proj_bc], axis=1)
    conv_taps = conv_x.shape[0]
    rim_rows = passed_along(mixed_in[tok_rows - conv_taps + 1 :], "ctx", 1)
    kernel = jnp.concatenate([conv_x, conv_bc.reshape(conv_taps, 2 * group_cols)], axis=1)
    extended = jnp.concatenate([rim_rows, mixed_in], axis=0)
    convolved = jnp.zeros_like(mixed_in)
    for offset in range(conv_taps):
        convolved = convolved + kernel[offset] * extended[offset : offset + tok_rows]
    activated = jax.nn.silu(convolved)
    heads = step_raw.shape[1]
    x_heads = activated[:, :channels].reshape(tok_rows, heads, HEAD_DIM)
    b_act = activated[:, channels : channels + group_cols]
    c_act = activated[:, channels + group_cols :]
    step_size = jax.nn.softplus(step_raw + dt_bias)
    log_rate = -jnp.exp(a_log) * step_size
    positions = jnp.arange(tok_rows)
    causal = positions[:, None] >= positions[None, :]
    log_decay = jnp.dot(causal.astype(f32), log_rate, precision=exact_prec)
    log_total = log_decay[-1]

    tail_decay = jnp.exp(log_total[None, :] - log_decay) * step_size
    end_state = jnp.einsum("sh,shp,sn->hpn", tail_decay, x_heads, b_act, precision=exact_prec)
    part_rows = heads * HEAD_DIM // ctx_count
    slices = end_state.astype(bf16).reshape(ctx_count, part_rows, STATE)
    first = log_total.astype(bf16)
    second = (log_total - first.astype(f32)).astype(bf16)
    third = (log_total - first.astype(f32) - second.astype(f32)).astype(bf16)
    totals = jnp.repeat(jnp.stack([first, second, third], axis=1), ctx_count // heads, axis=0)
    totals = jnp.broadcast_to(totals[:, :, None], (ctx_count, 3, STATE))
    totals = jnp.concatenate([totals, jnp.zeros((ctx_count, 13, STATE), bf16)], axis=1)
    message = jnp.concatenate([slices, totals], axis=1)
    arrived = lax.all_to_all(message, "ctx", 0, 0, tiled=True)
    decay_gap = log_decay.T[:, :, None] - log_decay.T[:, None, :]
    decay_mask = jnp.exp(jnp.where(causal[None], decay_gap, -jnp.inf))
    scores = jnp.einsum("tn,sn->ts", c_act, b_act, precision=exact_prec)
    mixing = scores[None] * decay_mask * step_size.T[:, None, :]
    y_local = jnp.einsum("hts,shp->thp", mixing, x_heads, precision=exact_prec)
    y_local = y_local + d_skip[None, :, None] * x_heads
    arrived, y_local, w_out_full = lax.optimization_barrier((arrived, y_local, w_out_full))
    block_logs = jnp.sum(arrived[:, part_rows : part_rows + 3, 0].astype(f32), axis=1)
    blocks = jnp.arange(ctx_count)
    earlier = blocks[:, None] > blocks[None, :]
    upto = jnp.sum(jnp.where(blocks[:, None] >= blocks[None, :], block_logs[None, :], 0.0), axis=1)
    gap = (upto - block_logs)[:, None] - upto[None, :]
    weigh = jnp.exp(jnp.where(earlier, gap, -jnp.inf))
    parts = arrived[:, :part_rows].astype(f32).reshape(ctx_count, part_rows * STATE)
    entering = jnp.dot(weigh, parts, precision=exact_prec).astype(bf16)
    entering = entering.reshape(ctx_count, part_rows, STATE)
    state_in = lax.all_to_all(entering, "ctx", 0, 0, tiled=True)
    state_in = state_in.reshape(heads, HEAD_DIM, STATE).astype(f32)

    y_carry = (
        jnp.einsum("tn,hpn->thp", c_act, state_in, precision=exact_prec)
        * jnp.exp(log_decay)[:, :, None]
    )
    mixer_out = y_local + y_carry
    gated_raw = mixer_out.reshape(tok_rows, channels) * jax.nn.silu(gate_z)
    gated_out = rms_scale(gated_raw, norm_gain).astype(bf16)

    partial_out = project_out(gated_out, w_out_full, head_at)
    partial_out, vocab_own = lax.optimization_barrier((partial_out, vocab_own))
    vocab_other = swap_core(vocab_own)
    summed_out = ring_reduce([partial_out[k] for k in range(4)], shift_head)
    residual = (own_emb.astype(f32) + summed_out).astype(bf16)
    normed_out = rms_scale(residual.astype(f32), final_gain).astype(bf16)

    along_first, along_second = shift_mixed(True), shift_mixed(False)
    from_left = moved(normed_out, along_first, 1)
    from_right = moved(normed_out, along_first, -1)
    from_far = moved(normed_out, along_first, 2)
    near = jnp.concatenate([normed_out, from_left])
    rest = jnp.concatenate([from_right, from_far])
    near_left = moved(near, along_second, 1)
    near_right = moved(near, along_second, -1)
    rest_left = moved(rest, along_second, 1)
    rest_right = moved(rest, along_second, -1)
    y_pos, z_pos, core = ctx_pos // 8, (ctx_pos // 2) % 4, ctx_pos % 2
    by_chip = lax.dynamic_index_in_dim(group_targets.reshape(4, 4, 2, quarter), core, 2, False)
    by_chip = jnp.roll(by_chip, (-y_pos, -z_pos), (0, 1))
    by_chip = jnp.where(core == 0, by_chip, by_chip.transpose(1, 0, 2))
    order = (0, 3, 1, 2)
    by_chip = jnp.stack([by_chip[:, k] for k in order], axis=1).reshape(4, 1, 4 * quarter)
    vocab_width = vocab_own.shape[1]
    by_chip = jnp.stack([by_chip - ctx_pos * vocab_width, by_chip - (ctx_pos ^ 1) * vocab_width])
    tables = (vocab_own, vocab_other)
    rows = 4 * quarter
    near, near_left, rest_right = lax.optimization_barrier((near, near_left, rest_right))
    stats = [vocab_stats((near, rest), by_chip[:, 0], tables)]
    near_far = moved(near_left, along_second, 1)
    rest_far = moved(rest_right, along_second, -1)
    near_far, rest_far, stats[0] = lax.optimization_barrier((near_far, rest_far, stats[0]))
    aims = jnp.concatenate([by_chip[:, k] for k in (1, 2, 3)], axis=1)
    others = (near_right, rest_right, near_far, rest_far, near_left, rest_left)
    others = vocab_stats(others, aims, tables)
    for k in range(1, 4):
        stats.append(moved(others[:, (k - 1) * rows : k * rows], along_second, k))
    merged = tuple(stats[0][:5])
    for other in stats[1:]:
        merged = join_stats(merged, tuple(other[:5]))
    both = jnp.stack(merged).reshape(5, 4, quarter)
    merged = tuple(both[:, 0])
    for place in range(1, 4):
        merged = join_stats(merged, tuple(moved(both[:, place], along_first, order[place])))
    row_peak, exp_sum, first_moment, second_moment, target_logit = merged
    mean_shift = first_moment / exp_sum
    spread = second_moment / exp_sum - mean_shift * mean_shift
    return (target_logit - row_peak - mean_shift) * lax.rsqrt(jnp.maximum(spread, 0.25))


def solution(mesh):
    placed = (
        P("ctx"),
        P(("ctx", "head")),
        P("head", "ctx"),
        P(None, None, "head"),
        P(None, None, "head"),
        P(None, "head"),
        P(None, "head"),
        P(None, None, "head"),
        P("head"),
        P("head"),
        P("head"),
        P("head"),
        P(),
        P(),
        P("head", "ctx"),
        P("head", "ctx"),
    )
    return jax.shard_map(
        on_device, mesh=mesh, in_specs=placed, out_specs=P(("ctx", "head")), check_vma=False
    )
```
